256 devices in a mesh: front: 16 (over z, core), row: 4 (over x), col: 4 (over y).
Axes of the slice: x: 4, y: 4, z: 8, core: 2. Of those that a mesh axis runs over, the one named last changes fastest.
Arguments:
- front: float32 [4, 128, 128, 4, 8, 128], P('row', 'front', None, 'col'), parts along dimension 1, as said below
- pattern: int32 [32, 32, 32], P('front'), parts along dimension 0, may hold values from 0 to 1, as said below
Outputs:
- factored: float32 [4, 128, 128, 4, 8, 128], P('row', 'front', None, 'col'), parts along dimension 1
The draws below stay inside these ranges and needn't reach their ends.
There are 16 independent parts, one for each index of `front`. The reference program is written for one: setup_inputs(seed, part) draws one part's arguments, and reference() takes and returns one part's arrays. A program takes and returns all parts, laid end to end along the dimension named above; each array names one. Nothing has to cross between parts.
Inputs may be any that keep to these rules, and one draw needn't show every extreme that they name: `pattern`: 0 or 1; symmetric in the two block indices; 1 on the block diagonal and on every block pair whose two block indices are both below 8. `front`: symmetric positive definite.
All inputs are finite; a program needn't handle non-finite values.
Results may differ from the reference program's by a relative error of at most 0.0001.
Values sent between devices are 32-bit elements; how exact they have to be, the bound alone decides.
No kernel may reach another device: no remote copies, remote signals or barrier semaphores. Data moves between devices by JAX's collectives and lax.ppermute only.
A program may use at most 128 MiB of HBM per device.

```python
import jax
import jax.numpy as jnp
from jax import lax

BS = 128
PANEL = 512
NPAN = 2
LB = 8
NBLK = 32
ORDER = 4096
N_ROW = 4
N_COL = 4


def draw_front(key, part):
    key = jax.random.fold_in(key, 11)
    first = jax.random.fold_in(key, 0)
    second = jax.random.fold_in(key, 1)
    fourth = jax.random.fold_in(key, 3)
    base = jax.random.truncated_normal(first, -4.0, 4.0, (ORDER, ORDER), jnp.float32)
    sym = (base + base.T) * (0.5 / ORDER ** 0.5)
    diag_vals = jax.random.uniform(second, (ORDER,), jnp.float32, 1.6, 2.4)
    common = jax.random.uniform(fourth, (ORDER,), jnp.float32, 0.5, 1.5)
    coupling = 2.0 / ORDER ** 0.5 * common[:, None] * common[None, :]
    dense = sym + jnp.diag(diag_vals) + coupling
    return jnp.transpose(dense.reshape(LB, N_ROW, BS, LB, N_COL, BS), (1, 0, 2, 4, 3, 5))


def draw_pattern(key, part):
    key = jax.random.fold_in(key, 12)
    first, second = jax.random.split(key)
    weights = jax.random.randint(first, (NBLK,), 1, 5)
    picks = jax.random.randint(second, (NPAN, NBLK, NBLK), 0, 100)
    marks = (picks < weights[:, None] * weights[None, :]).astype(jnp.int32)
    marks = jnp.maximum(marks, jnp.swapaxes(marks, 1, 2))
    marks = jnp.maximum(marks, jnp.eye(NBLK, dtype=jnp.int32)[None])
    ids = jnp.arange(NBLK)
    limit = NPAN * (PANEL // BS)
    inner = ((ids[:, None] < limit) & (ids[None, :] < limit)).astype(jnp.int32)
    marks = jnp.maximum(marks, inner[None])
    return marks.astype(jnp.int32)


def setup_inputs(seed: int = 0, part: int = 0) -> dict:
    keys = jax.random.split(jax.random.key(seed), 3)
    part_splits = jax.random.split(jax.random.fold_in(keys[2], part), 3)
    return {
        "front": draw_front(jax.random.fold_in(jax.random.fold_in(keys[2], part), 71), part),
        "pattern": draw_pattern(jax.random.fold_in(jax.random.fold_in(keys[2], part), 71), part),
    }


def reference(front, pattern):
    dense = jnp.transpose(front, (1, 0, 2, 4, 3, 5)).reshape(ORDER, ORDER)
    block_ids = jnp.arange(NBLK)
    glob = jnp.arange(ORDER)
    factors = []
    for k in range(NPAN):
        start = k * PANEL
        corner = dense[start:start + PANEL, start:start + PANEL]
        lower = jnp.linalg.cholesky(corner)
        strip = dense[:, start:start + PANEL]
        rows = lax.linalg.triangular_solve(lower, strip, left_side=False, lower=True, transpose_a=True)
        rows = jnp.where(glob[:, None] >= start + jnp.arange(PANEL)[None, :], rows, 0.0)
        factors.append(rows)
        edge = (k + 1) * (PANEL // BS)
        live = (pattern[k] > 0) & (block_ids[:, None] >= edge) & (block_ids[None, :] >= edge)
        live = jnp.repeat(jnp.repeat(live, BS, 0), BS, 1)
        update = jnp.dot(rows, rows.T, precision=lax.Precision.HIGHEST)
        dense = dense - jnp.where(live, update, 0.0)
    done = NPAN * PANEL
    result = dense
    for k in range(NPAN):
        result = result.at[:, k * PANEL:(k + 1) * PANEL].set(factors[k])
    upper_zone = (glob[:, None] < done) & (glob[None, :] >= done)
    result = jnp.where(upper_zone, 0.0, result)
    return jnp.transpose(result.reshape(LB, N_ROW, BS, LB, N_COL, BS), (1, 0, 2, 4, 3, 5))
```

```python
import functools

import jax
import jax.numpy as jnp
from jax import lax
from jax.experimental import pallas as pl
from jax.experimental.pallas import tpu as pltpu
from jax.sharding import PartitionSpec as P

F32 = jnp.float32
BF16 = jnp.bfloat16
HI = lax.Precision.HIGHEST
EDGE = 128
TILE = 8
GROUPS = 4
WIDTH = EDGE * GROUPS
LB = 8
NPAN = 2
REST = LB - NPAN
ROWS = REST * EDGE
LIMIT = 60 * 1024 * 1024

NN = (((1,), (0,)), ((), ()))
NT = (((1,), (1,)), ((), ()))
TN = (((0,), (0,)), ((), ()))


def exact_dot(a, b, dims):
    return lax.dot_general(a, b, dims, precision=HI, preferred_element_type=F32)


def split2(x):
    high = x.astype(BF16)
    return high, (x - high.astype(F32)).astype(BF16)


def split3(x):
    high, rest = x.astype(BF16), None
    rest = x - high.astype(F32)
    mid = rest.astype(BF16)
    return high, mid, (rest - mid.astype(F32)).astype(BF16)


def dot3(a, b, dims):
    one = functools.partial(lax.dot_general, dimension_numbers=dims, preferred_element_type=F32)
    return one(a[0], b[0]) + (one(a[0], b[1]) + one(a[1], b[0]))


def factor_block(a, w):
    sub = lax.broadcasted_iota(jnp.int32, (TILE, EDGE), 0)
    for p in range(EDGE // TILE):
        at = slice(TILE * p, TILE * (p + 1))
        left, right = a[at, :], w[at, :]
        cols = [jnp.broadcast_to(left[:, TILE * p + q:TILE * p + q + 1], (TILE, EDGE)) for q in range(TILE)]
        invs = jnp.zeros((TILE, EDGE), F32)
        for q in range(TILE):
            inv = 1.0 / jnp.broadcast_to(cols[q][q:q + 1, :], (TILE, EDGE))
            m = jnp.where(sub > q, cols[q] * inv, 0.0)
            invs = jnp.where(sub == q, inv, invs)
            left = left - m * jnp.broadcast_to(left[q:q + 1, :], (TILE, EDGE))
            right = right - m * jnp.broadcast_to(right[q:q + 1, :], (TILE, EDGE))
            for t in range(q + 1, TILE):
                cols[t] = cols[t] - m * jnp.broadcast_to(cols[t][q:q + 1, :], (TILE, EDGE))
        root = lax.rsqrt(invs) * invs
        left, right = left * root, right * root
        a[at, :], w[at, :] = left, right
        low = TILE * (p + 1)
        if low < EDGE:
            h, m, l = split3(left)
            vh, vm, vl = split3(right)
            uh, um, ul = (jnp.concatenate(pair, 1) for pair in ((h, vh), (m, vm), (l, vl)))
            lhs = jnp.concatenate([h, h, m, h, m, l], 0)
            rhs = jnp.concatenate([uh, um, uh, ul, um, uh], 0)
            change = lax.dot_general(lhs, rhs, TN, preferred_element_type=F32)
            a[low:, :] = a[low:, :] - change[low:, :EDGE]
            w[low:, :] = w[low:, :] - change[low:, EDGE:]


def factor_panel(s, lower, inverse, a, w):
    ri = lax.broadcasted_iota(jnp.int32, (EDGE, EDGE), 0)
    ci = lax.broadcasted_iota(jnp.int32, (EDGE, EDGE), 1)
    lower[...] = jnp.zeros((WIDTH, WIDTH), F32)
    inverse[...] = jnp.zeros((WIDTH, WIDTH), F32)

    def step(i, _):
        at = pl.ds(pl.multiple_of(i * EDGE, EDGE), EDGE)
        a[...] = s[at, at]
        w[...] = jnp.where(ri == ci, 1.0, 0.0)
        factor_block(a, w)
        lower[at, at] = jnp.where(ri <= ci, a[...], 0.0).T
        d = w[...]
        inverse[at, at] = d
        for k in range(GROUPS):
            here = slice(k * EDGE, (k + 1) * EDGE)
            below = slice((k + 1) * EDGE, WIDTH)
            before = slice(0, k * EDGE)

            @pl.when(i == k)
            def _():
                if k + 1 < GROUPS:
                    part = exact_dot(s[below, here], d, NT)
                    lower[below, here] = part
                    s[below, below] = s[below, below] - exact_dot(part, part, NT)
                if k > 0:
                    part = exact_dot(lower[here, before], inverse[before, before], NN)
                    inverse[here, before] = -exact_dot(d, part, NN)
        return 0

    lax.fori_loop(0, GROUPS, step, 0)


def first_kernel(got, lower, inverse, s, a, w):
    for r in range(GROUPS):
        for c in range(r + 1):
            s[r * EDGE:(r + 1) * EDGE, c * EDGE:(c + 1) * EDGE] = got[r * GROUPS + c]
    factor_panel(s, lower, inverse, a, w)


def second_kernel(got, inverse0, across, lower, inverse, s, a, w):
    for r in range(GROUPS):
        for c in range(GROUPS):
            s[r * EDGE:(r + 1) * EDGE, c * EDGE:(c + 1) * EDGE] = got[r * GROUPS + c, 0]
    across[...] = exact_dot(s[...], inverse0[...], NT)
    for r in range(GROUPS):
        for c in range(r + 1):
            s[r * EDGE:(r + 1) * EDGE, c * EDGE:(c + 1) * EDGE] = got[r * GROUPS + c, 1]
    s[...] = s[...] - exact_dot(across[...], across[...], NT)
    factor_panel(s, lower, inverse, a, w)


def last_kernel(front, pattern, ar, ac, low0, inv0, across, low1, inv1, out, xh, xl, yh, yl, lr, lc):
    r, c = lax.axis_index("row"), lax.axis_index("col")
    own = pl.ds(pl.multiple_of(c * EDGE, EDGE), EDGE)
    mine = pl.ds(pl.multiple_of(r * EDGE, EDGE), EDGE)
    zero = jnp.zeros((EDGE, EDGE), F32)
    for l in range(NPAN):
        for m in range(NPAN, LB):
            out[l, :, m, :] = zero
    out[0, :, 1, :] = zero
    out[0, :, 0, :] = low0[mine, own]
    out[1, :, 0, :] = across[mine, own]
    out[1, :, 1, :] = low1[mine, own]
    for k in range(NPAN):
        for g in range(GROUPS):
            span = slice(g * EDGE, (g + 1) * EDGE)
            if k == 0:
                xh[:, span], xl[:, span] = split2(ar[g, k])
                yh[span, :], yl[span, :] = split2(ac[g, k])
            else:
                block = split2(across[span, :])
                lr[:, span] = ar[g, k]
                lc[span, :] = ac[g, k]
                for l in range(REST):
                    rows = slice(l * EDGE, (l + 1) * EDGE)

                    @pl.when(pattern[0, (l + NPAN) * GROUPS + r, GROUPS + g] > 0)
                    def _():
                        lr[rows, span] = lr[rows, span] - dot3((xh[rows, :], xl[rows, :]), block, NT)

                    @pl.when(pattern[0, GROUPS + g, (l + NPAN) * GROUPS + c] > 0)
                    def _():
                        lc[span, rows] = lc[span, rows] - dot3(block, (yh[:, rows], yl[:, rows]), NN)
        if k == 1:
            xh[...], xl[...] = split2(lr[...])
            yh[...], yl[...] = split2(lc[...])
        inv = split2((inv0, inv1)[k][...])
        lr[...] = dot3((xh[...], xl[...]), inv, NT)
        lc[...] = dot3(inv, (yh[...], yl[...]), NN)
        xh[...], xl[...] = split2(lr[...])
        yh[...], yl[...] = split2(lc[...])
        for l in range(REST):
            rows = slice(l * EDGE, (l + 1) * EDGE)
            out[l + NPAN, :, k, :] = lr[rows, own]
            for m in range(REST):
                cols = slice(m * EDGE, (m + 1) * EDGE)
                if k == 0:
                    out[l + NPAN, :, m + NPAN, :] = front[l + NPAN, :, m + NPAN, :]

                @pl.when(pattern[k, (l + NPAN) * GROUPS + r, (m + NPAN) * GROUPS + c] > 0)
                def _():
                    out[l + NPAN, :, m + NPAN, :] = out[l + NPAN, :, m + NPAN, :] - dot3(
                        (xh[rows, :], xl[rows, :]), (yh[:, cols], yl[:, cols]), NN)


def extract_kernel(front, ar, ac):
    for k in range(NPAN):
        for j in range(REST):
            span = slice(j * EDGE, (j + 1) * EDGE)
            ar[k, span, :] = front[j + NPAN, :, k, :]
            ac[k, :, span] = front[k, :, j + NPAN, :]


def corner_kernel(front, c0, c1):
    c0[...] = front[0, :, 0, :]
    c1[0] = front[1, :, 0, :]
    c1[1] = front[1, :, 1, :]


def shape(*dims):
    return jax.ShapeDtypeStruct(dims, F32)


def vmem(*dims, dtype=F32):
    return pltpu.VMEM(dims, dtype)


def call(kernel, outs, scratch=(), **kw):
    return pl.pallas_call(
        kernel, out_shape=outs, scratch_shapes=list(scratch),
        compiler_params=pltpu.CompilerParams(vmem_limit_bytes=LIMIT), **kw)


def everyone(x):
    full = jnp.broadcast_to(x[None], (GROUPS * GROUPS,) + x.shape)
    return lax.all_to_all(full, ("row", "col"), 0, 0, tiled=True)


def per_device(front, pattern):
    blocks = front[0, :, :, 0]
    work = [vmem(WIDTH, WIDTH), vmem(EDGE, EDGE), vmem(EDGE, EDGE)]
    square = shape(WIDTH, WIDTH)
    c0, c1 = call(
        corner_kernel, [shape(EDGE, EDGE), shape(2, EDGE, EDGE)], grid=(1,),
        in_specs=[pl.BlockSpec((NPAN, EDGE, LB, EDGE), lambda i: (0, 0, 0, 0))],
        out_specs=[pl.BlockSpec((EDGE, EDGE), lambda i: (0, 0)), pl.BlockSpec((2, EDGE, EDGE), lambda i: (0, 0, 0))],
    )(blocks)
    ar, ac = call(extract_kernel, [shape(NPAN, ROWS, EDGE), shape(NPAN, EDGE, ROWS)])(blocks)
    got0 = everyone(c0)
    got1 = everyone(c1)
    ar = lax.all_gather(ar, "col", axis=0)
    ac = lax.all_gather(ac, "row", axis=0)
    low0, inv0 = call(first_kernel, [square] * 2, work)(got0)
    across, low1, inv1 = call(second_kernel, [square] * 3, work)(got1, inv0)
    whole = pl.BlockSpec(memory_space=pltpu.VMEM)
    result = call(
        last_kernel, shape(LB, EDGE, LB, EDGE),
        [vmem(ROWS, WIDTH, dtype=BF16)] * 2 + [vmem(WIDTH, ROWS, dtype=BF16)] * 2 + [vmem(ROWS, WIDTH), vmem(WIDTH, ROWS)],
        in_specs=[whole, pl.BlockSpec(memory_space=pltpu.SMEM)] + [whole] * 7,
        out_specs=whole,
    )(blocks, pattern, ar, ac, low0, inv0, across, low1, inv1)
    return result[None, :, :, None]


def solution(mesh):
    placed = (P("row", "front", None, "col", None, None), P("front", None, None))
    return jax.shard_map(
        per_device, mesh=mesh, in_specs=placed,
        out_specs=P("row", "front", None, "col", None, None), check_vma=False,
    )
```

```python
import functools

import jax
import jax.numpy as jnp
from jax import lax
from jax.experimental import pallas as pl
from jax.experimental.pallas import tpu as pltpu
from jax.sharding import PartitionSpec as P

F32 = jnp.float32
BF16 = jnp.bfloat16
HI = lax.Precision.HIGHEST
EDGE = 128
TILE = 8
GROUPS = 4
WIDTH = EDGE * GROUPS
LB = 8
NPAN = 2
REST = LB - NPAN
ROWS = REST * EDGE

NN = (((1,), (0,)), ((), ()))
NT = (((1,), (1,)), ((), ()))
TN = (((0,), (0,)), ((), ()))


def exact_dot(a, b, dims):
    return lax.dot_general(a, b, dims, precision=HI, preferred_element_type=F32)


def split2(x):
    high = x.astype(BF16)
    return high, (x - high.astype(F32)).astype(BF16)


def split3(x):
    high = x.astype(BF16)
    rest = x - high.astype(F32)
    mid = rest.astype(BF16)
    return high, mid, (rest - mid.astype(F32)).astype(BF16)


def dot3(a, b, dims):
    one = functools.partial(lax.dot_general, dimension_numbers=dims, preferred_element_type=F32)
    return one(a[0], b[0]) + (one(a[0], b[1]) + one(a[1], b[0]))


def spread(x):
    return jnp.broadcast_to(x, (TILE, EDGE))


def factor_block(a, w):
    sub = lax.broadcasted_iota(jnp.int32, (TILE, EDGE), 0)
    count = EDGE // TILE
    left, right = a[:TILE, :], w[:TILE, :]
    for p in range(count):
        at, after = slice(TILE * p, TILE * (p + 1)), slice(TILE * (p + 1), TILE * (p + 2))
        more = p + 1 < count
        cols = [spread(left[:, TILE * p + q:TILE * p + q + 1]) for q in range(TILE)]
        if more:
            next_left, next_right = a[after, :], w[after, :]
            next_cols = [spread(next_left[:, TILE * p + q:TILE * p + q + 1]) for q in range(TILE)]
        invs = jnp.zeros((TILE, EDGE), F32)
        pivot = spread(cols[0][:1, :])
        for q in range(TILE):
            inv = 1.0 / pivot
            if q + 1 < TILE:
                beside = spread(cols[q + 1][q:q + 1, :])
                pivot = spread(cols[q + 1][q + 1:q + 2, :]) - (beside * beside) * inv
            m = jnp.where(sub > q, cols[q], 0.0) * inv
            invs = jnp.where(sub == q, inv, invs)
            row_left, row_right = spread(left[q:q + 1, :]), spread(right[q:q + 1, :])
            left, right = left - m * row_left, right - m * row_right
            if more:
                n = next_cols[q] * inv
                next_left, next_right = next_left - n * row_left, next_right - n * row_right
            for t in range(q + 1, TILE):
                across = spread(cols[t][q:q + 1, :])
                cols[t] = cols[t] - m * across
                if more:
                    next_cols[t] = next_cols[t] - n * across
        root = lax.rsqrt(invs) * invs
        left, right = left * root, right * root
        a[at, :], w[at, :] = left, right
        low = TILE * (p + 2)
        if low < EDGE:
            h, m, l = split3(left)
            vh, vm, vl = split3(right)
            uh, um, ul = (jnp.concatenate(pair, 1) for pair in ((h, vh), (m, vm), (l, vl)))
            lhs = jnp.concatenate([h, h, m, h, m, l], 0)
            rhs = jnp.concatenate([uh, um, uh, ul, um, uh], 0)
            change = lax.dot_general(lhs, rhs, TN, preferred_element_type=F32)
            a[low:, :] = a[low:, :] - change[low:, :EDGE]
            w[low:, :] = w[low:, :] - change[low:, EDGE:]
        if more:
            left, right = next_left, next_right


def factor_panel(s, lower, inverse, a, w):
    ri = lax.broadcasted_iota(jnp.int32, (EDGE, EDGE), 0)
    ci = lax.broadcasted_iota(jnp.int32, (EDGE, EDGE), 1)
    lower[...] = jnp.zeros((WIDTH, WIDTH), F32)
    inverse[...] = jnp.zeros((WIDTH, WIDTH), F32)

    def step(i, _):
        at = pl.ds(pl.multiple_of(i * EDGE, EDGE), EDGE)
        a[...] = s[at, at]
        w[...] = jnp.where(ri == ci, 1.0, 0.0)
        factor_block(a, w)
        lower[at, at] = jnp.where(ri <= ci, a[...], 0.0).T
        d = w[...]
        inverse[at, at] = d
        for k in range(GROUPS):
            here = slice(k * EDGE, (k + 1) * EDGE)
            below = slice((k + 1) * EDGE, WIDTH)
            before = slice(0, k * EDGE)

            @pl.when(i == k)
            def _():
                if k + 1 < GROUPS:
                    part = exact_dot(s[below, here], d, NT)
                    lower[below, here] = part
                    s[below, below] = s[below, below] - exact_dot(part, part, NT)
                if k > 0:
                    part = exact_dot(lower[here, before], inverse[before, before], NN)
                    inverse[here, before] = -exact_dot(d, part, NN)
        return 0

    lax.fori_loop(0, GROUPS, step, 0)


def first_kernel(got, lower, inverse, s, a, w):
    for r in range(GROUPS):
        for c in range(r + 1):
            s[r * EDGE:(r + 1) * EDGE, c * EDGE:(c + 1) * EDGE] = got[r * GROUPS + c]
    factor_panel(s, lower, inverse, a, w)


def second_kernel(got, inverse0, across, lower, inverse, s, a, w):
    for r in range(GROUPS):
        for c in range(GROUPS):
            s[r * EDGE:(r + 1) * EDGE, c * EDGE:(c + 1) * EDGE] = got[r * GROUPS + c, 0]
    across[...] = dot3(split2(s[...]), split2(inverse0[...]), NT)
    for r in range(GROUPS):
        for c in range(r + 1):
            s[r * EDGE:(r + 1) * EDGE, c * EDGE:(c + 1) * EDGE] = got[r * GROUPS + c, 1]
    part = split2(across[...])
    s[...] = s[...] - dot3(part, part, NT)
    factor_panel(s, lower, inverse, a, w)


def last_kernel(front, pattern, ar, ac0, ac1, ac3, ac2, low0, inv0, across, low1, inv1, out,
                buf, arv, acv, xh, xl, yh, yl, bh, bl, lr, lc, arrive, leave):
    r, c = lax.axis_index("row"), lax.axis_index("col")
    own = pl.ds(pl.multiple_of(c * EDGE, EDGE), EDGE)
    mine = pl.ds(pl.multiple_of(r * EDGE, EDGE), EDGE)
    half = WIDTH // 2
    loads = []
    for k in range(NPAN):
        loads.append(pltpu.make_async_copy(ar.at[:, k], arv.at[:, k], arrive.at[8 * k]))
        for s, ac in ((0, ac0), (1, ac1), (2, ac2), (3, ac3)):
            loads.append(pltpu.make_async_copy(ac.at[k], acv.at[(r + GROUPS - s) % GROUPS, k], arrive.at[8 * k + s + 1]))
    fronts = [pltpu.make_async_copy(front.at[l], buf.at[l], arrive.at[16 + l]) for l in range(NPAN, LB)]
    for load in loads + fronts:
        load.start()
    stores = [pltpu.make_async_copy(buf.at[l], out.at[l], leave.at[l]) for l in range(LB)]
    zero = jnp.zeros((EDGE, EDGE), F32)
    for l in range(NPAN):
        for m in range(NPAN, LB):
            buf[l, :, m, :] = zero
    buf[0, :, 1, :] = zero
    buf[0, :, 0, :] = low0[mine, own]
    buf[1, :, 0, :] = across[mine, own]
    buf[1, :, 1, :] = low1[mine, own]
    stores[0].start()
    stores[1].start()
    bh[...], bl[...] = split2(across[...])

    def spans(i):
        return pl.ds(pl.multiple_of(i * EDGE, EDGE), EDGE)

    for k in range(NPAN):
        for load in loads[5 * k:5 * k + 5]:
            load.wait()
        if k == 0:
            for g in range(GROUPS):
                span = slice(g * EDGE, (g + 1) * EDGE)
                xh[:, span], xl[:, span] = split2(arv[g, k].reshape(ROWS, EDGE))
                yh[span, :], yl[span, :] = split2(acv[g, k])
        else:
            for g in range(GROUPS):
                span = slice(g * EDGE, (g + 1) * EDGE)
                lr[:, span] = arv[g, k].reshape(ROWS, EDGE)
                lc[span, :] = acv[g, k]

            def row_side(l, _):
                rows = spans(l)
                for g in range(GROUPS):
                    span = slice(g * EDGE, (g + 1) * EDGE)

                    @pl.when(pattern[0, (l + NPAN) * GROUPS + r, GROUPS + g] > 0)
                    def _():
                        lr[rows, span] = lr[rows, span] - dot3(
                            (xh[rows, :], xl[rows, :]), (bh[span, :], bl[span, :]), NT)
                return 0

            def col_side(g, _):
                span = spans(g)
                for l in range(REST):
                    cols = slice(l * EDGE, (l + 1) * EDGE)

                    @pl.when(pattern[0, GROUPS + g, (l + NPAN) * GROUPS + c] > 0)
                    def _():
                        lc[span, cols] = lc[span, cols] - dot3(
                            (bh[span, :], bl[span, :]), (yh[:, cols], yl[:, cols]), NN)
                return 0

            lax.fori_loop(0, REST, row_side, 0)
            lax.fori_loop(0, GROUPS, col_side, 0)
            xh[...], xl[...] = split2(lr[...])
            yh[...], yl[...] = split2(lc[...])
        wh, wl = split2((inv0, inv1)[k][...])
        lr[:, :half] = dot3((xh[:, :half], xl[:, :half]), (wh[:half, :half], wl[:half, :half]), NT)
        lr[:, half:] = dot3((xh[...], xl[...]), (wh[half:, :], wl[half:, :]), NT)
        lc[:half, :] = dot3((wh[:half, :half], wl[:half, :half]), (yh[:half, :], yl[:half, :]), NN)
        lc[half:, :] = dot3((wh[half:, :], wl[half:, :]), (yh[...], yl[...]), NN)
        xh[...], xl[...] = split2(lr[...])
        yh[...], yl[...] = split2(lc[...])
        if k == 0:
            for load in fronts:
                load.wait()

        def update(l, _):
            rows = spans(l)
            buf[l + NPAN, :, k, :] = lr[rows, own]
            for m in range(REST):
                cols = slice(m * EDGE, (m + 1) * EDGE)

                @pl.when(pattern[k, (l + NPAN) * GROUPS + r, (m + NPAN) * GROUPS + c] > 0)
                def _():
                    buf[l + NPAN, :, m + NPAN, :] = buf[l + NPAN, :, m + NPAN, :] - dot3(
                        (xh[rows, :], xl[rows, :]), (yh[:, cols], yl[:, cols]), NN)
            return 0

        lax.fori_loop(0, REST, update, 0)
    for store in stores[NPAN:]:
        store.start()
    for store in stores:
        store.wait()


def run(copies):
    for copy in copies:
        copy.start()
    for copy in copies:
        copy.wait()


def extract_kernel(front, ar, ac, rows, cols, sem):
    copy = pltpu.make_async_copy
    loads = [copy(front.at[NPAN:, :, k, :], rows.at[k], sem.at[k]) for k in range(NPAN)]
    for k in range(NPAN):
        for j in range(REST):
            loads.append(copy(front.at[k, :, j + NPAN, :], cols.at[k, :, j * EDGE:(j + 1) * EDGE], sem.at[len(loads)]))
    run(loads)
    run([copy(rows, ar, sem.at[0]), copy(cols, ac, sem.at[1])])


def corner_kernel(front, c0, c1, first, second, sem):
    copy = pltpu.make_async_copy
    every = GROUPS * GROUPS
    load = copy(front.at[0, :, 0, :], first, sem.at[0])
    more = [copy(front.at[1, :, m, :], second.at[m], sem.at[m + 1]) for m in range(2)]
    for one in [load] + more:
        one.start()
    load.wait()
    stores = [copy(first, c0.at[g], sem.at[3 + g]) for g in range(every)]
    for one in stores:
        one.start()
    for one in more:
        one.wait()
    last = [copy(second, c1.at[g], sem.at[3 + every + g]) for g in range(every)]
    for one in last:
        one.start()
    for one in stores + last:
        one.wait()


def shape(*dims):
    return jax.ShapeDtypeStruct(dims, F32)


def vmem(*dims, dtype=F32):
    return pltpu.VMEM(dims, dtype)


def call(kernel, outs, scratch=(), limit=60, **kw):
    return pl.pallas_call(
        kernel, out_shape=outs, scratch_shapes=list(scratch),
        compiler_params=pltpu.CompilerParams(vmem_limit_bytes=limit * 1024 * 1024), **kw)


def per_device(front, pattern):
    blocks = front[0, :, :, 0]
    work = [vmem(WIDTH, WIDTH), vmem(EDGE, EDGE), vmem(EDGE, EDGE)]
    square = shape(WIDTH, WIDTH)
    every = GROUPS * GROUPS
    away, dma = pl.BlockSpec(memory_space=pltpu.HBM), pltpu.SemaphoreType.DMA
    c0, c1 = call(
        corner_kernel, [shape(every, EDGE, EDGE), shape(every, 2, EDGE, EDGE)],
        [vmem(EDGE, EDGE), vmem(2, EDGE, EDGE), dma((3 + 2 * every,))],
        in_specs=[away], out_specs=[away, away],
    )(blocks)
    later, c0 = lax.optimization_barrier((blocks, c0))
    got0 = lax.all_to_all(c0, ("row", "col"), 0, 0, tiled=True)
    ar, ac = call(
        extract_kernel, [shape(NPAN, REST, EDGE, EDGE), shape(NPAN, EDGE, ROWS)],
        [vmem(NPAN, REST, EDGE, EDGE), vmem(NPAN, EDGE, ROWS), dma((NPAN + NPAN * REST,))],
        in_specs=[away], out_specs=[away, away],
    )(later)
    ar = lax.all_gather(ar, "col", axis=0)
    acs = [ac] + [lax.ppermute(ac, "row", [(i, (i + s) % GROUPS) for i in range(GROUPS)]) for s in (1, 3, 2)]
    c1, got0 = lax.optimization_barrier((c1, got0))
    got1 = lax.all_to_all(c1, ("row", "col"), 0, 0, tiled=True)
    low0, inv0 = call(first_kernel, [square] * 2, work)(got0)
    across, low1, inv1 = call(second_kernel, [square] * 3, work)(got1, inv0)
    whole = pl.BlockSpec(memory_space=pltpu.VMEM)
    result = call(
        last_kernel, shape(LB, EDGE, LB, EDGE),
        [vmem(LB, EDGE, LB, EDGE), vmem(GROUPS, NPAN, REST, EDGE, EDGE), vmem(GROUPS, NPAN, EDGE, ROWS)]
        + [vmem(ROWS, WIDTH, dtype=BF16)] * 2 + [vmem(WIDTH, ROWS, dtype=BF16)] * 2 + [vmem(WIDTH, WIDTH, dtype=BF16)] * 2
        + [vmem(ROWS, WIDTH), vmem(WIDTH, ROWS), dma((24,)), dma((LB,))],
        in_specs=[away, pl.BlockSpec(memory_space=pltpu.SMEM), away, away, away, away, away] + [whole] * 5,
        out_specs=away,
    )(blocks, pattern, ar, *acs, low0, inv0, across, low1, inv1)
    return result[None, :, :, None]


def solution(mesh):
    placed = (P("row", "front", None, "col", None, None), P("front", None, None))
    return jax.shard_map(
        per_device, mesh=mesh, in_specs=placed,
        out_specs=P("row", "front", None, "col", None, None), check_vma=False,
    )
```

```python
import functools

import jax
import jax.numpy as jnp
from jax import lax
from jax.experimental import pallas as pl
from jax.experimental.pallas import tpu as pltpu
from jax.sharding import PartitionSpec as P

F32 = jnp.float32
BF16 = jnp.bfloat16
HI = lax.Precision.HIGHEST
EDGE = 128
TILE = 8
HALF = EDGE // 2
HELD = HALF + TILE
GROUPS = 4
WIDTH = EDGE * GROUPS
LB = 8
BATCH = 4
NPAN = 2
REST = LB - NPAN
ROWS = REST * EDGE

NN = (((1,), (0,)), ((), ()))
NT = (((1,), (1,)), ((), ()))
TN = (((0,), (0,)), ((), ()))


def exact_dot(a, b, dims):
    return lax.dot_general(a, b, dims, precision=HI, preferred_element_type=F32)


def split2(x):
    high = x.astype(BF16)
    return high, (x - high.astype(F32)).astype(BF16)


def split3(x):
    high = x.astype(BF16)
    rest = x - high.astype(F32)
    mid = rest.astype(BF16)
    return high, mid, (rest - mid.astype(F32)).astype(BF16)


def dot3(a, b, dims):
    one = functools.partial(lax.dot_general, dimension_numbers=dims, preferred_element_type=F32)
    return one(a[0], b[0]) + (one(a[0], b[1]) + one(a[1], b[0]))


def spread(x):
    return jnp.broadcast_to(x, (TILE, EDGE))


def factor_block(a, w):
    sub = lax.broadcasted_iota(jnp.int32, (TILE, EDGE), 0)
    count = EDGE // TILE
    left, right = a[:TILE, :], w[:TILE, :]
    for p in range(count):
        at, after = slice(TILE * p, TILE * (p + 1)), slice(TILE * (p + 1), TILE * (p + 2))
        more = p + 1 < count
        cols = [spread(left[:, TILE * p + q:TILE * p + q + 1]) for q in range(TILE)]
        if more:
            next_left, next_right = a[after, :], w[after, :]
            next_cols = [spread(next_left[:, TILE * p + q:TILE * p + q + 1]) for q in range(TILE)]
        invs = jnp.zeros((TILE, EDGE), F32)
        pivot = spread(cols[0][:1, :])
        for q in range(TILE):
            inv = 1.0 / pivot
            if q + 1 < TILE:
                beside = spread(cols[q + 1][q:q + 1, :])
                pivot = spread(cols[q + 1][q + 1:q + 2, :]) - (beside * beside) * inv
            m = jnp.where(sub > q, cols[q], 0.0) * inv
            invs = jnp.where(sub == q, inv, invs)
            row_left, row_right = spread(left[q:q + 1, :]), spread(right[q:q + 1, :])
            left, right = left - m * row_left, right - m * row_right
            if more:
                n = next_cols[q] * inv
                next_left, next_right = next_left - n * row_left, next_right - n * row_right
            for t in range(q + 1, TILE):
                across = spread(cols[t][q:q + 1, :])
                cols[t] = cols[t] - m * across
                if more:
                    next_cols[t] = next_cols[t] - n * across
        root = lax.rsqrt(invs) * invs
        left, right = left * root, right * root
        a[at, :], w[at, :] = left, right
        low = TILE * (p + 2)
        if low < EDGE:
            h, m, l = split3(left)
            vh, vm, vl = split3(right)
            uh, um, ul = (jnp.concatenate(pair, 1) for pair in ((h, vh), (m, vm), (l, vl)))
            lhs = jnp.concatenate([h, h, m, h, m, l], 0)
            rhs = jnp.concatenate([uh, um, uh, ul, um, uh], 0)
            change = lax.dot_general(lhs, rhs, TN, preferred_element_type=F32)
            a[low:, :] = a[low:, :] - change[low:, :EDGE]
            w[low:, :] = w[low:, :] - change[low:, EDGE:]
        if more:
            left, right = next_left, next_right


def factor_panel(s, lower, inverse, a, w):
    ri = lax.broadcasted_iota(jnp.int32, (EDGE, EDGE), 0)
    ci = lax.broadcasted_iota(jnp.int32, (EDGE, EDGE), 1)
    for k in range(GROUPS):
        here = slice(k * EDGE, (k + 1) * EDGE)
        below = slice((k + 1) * EDGE, WIDTH)
        before = slice(0, k * EDGE)
        a[k] = s[here, here]
        w[k] = jnp.where(ri == ci, 1.0, 0.0)
        factor_block(a.at[k], w.at[k])
        d = w[k]
        if k + 1 < GROUPS:
            part = exact_dot(s[below, here], d, NT)
            lower[below, here] = part
            s[below, below] = s[below, below] - exact_dot(part, part, NT)
            lower[here, below] = jnp.zeros((EDGE, WIDTH - (k + 1) * EDGE), F32)
            inverse[here, below] = jnp.zeros((EDGE, WIDTH - (k + 1) * EDGE), F32)
        lower[here, here] = jnp.where(ri <= ci, a[k], 0.0).T
        inverse[here, here] = d
        if k > 0:
            part = exact_dot(lower[here, before], inverse[before, before], NN)
            inverse[here, before] = -exact_dot(d, part, NN)


def pack(block, ref, r, c):
    row = lax.broadcasted_iota(jnp.int32, (HALF, EDGE), 0)
    lane = lax.broadcasted_iota(jnp.int32, (HALF, EDGE), 1)
    top, low = block[:HALF], block[HALF:]
    diagonal = jnp.where(lane - HALF > row, pltpu.roll(top, HALF, 1), low)
    ref[:HALF, :] = jnp.where(r == c, diagonal, jnp.where(r > c, top, block.T[HALF:]))
    ref[HALF:HELD, :] = spread(jnp.sum(jnp.where(lane == row, top, 0.0), axis=0, keepdims=True))


def unpack_diagonal(got):
    row = lax.broadcasted_iota(jnp.int32, (EDGE, EDGE), 0)
    lane = lax.broadcasted_iota(jnp.int32, (EDGE, EDGE), 1)
    body = got[:HALF]
    some = jnp.concatenate([pltpu.roll(body, HALF, 1), body], 0)
    kept = ((row >= HALF) & (lane <= row)) | ((lane < HALF) & (row < lane))
    whole = jnp.where(kept, some, some.T)
    return jnp.where((row == lane) & (row < HALF), jnp.broadcast_to(got[HALF:HALF + 1], (EDGE, EDGE)), whole)


def unpack(got, at, s):
    for r in range(GROUPS):
        for c in range(r):
            span = slice(c * EDGE, (c + 1) * EDGE)
            s[r * EDGE:r * EDGE + HALF, span] = got[r * GROUPS + c, at:at + HALF]
            s[r * EDGE + HALF:(r + 1) * EDGE, span] = got[c * GROUPS + r, at:at + HALF]
        span = slice(r * EDGE, (r + 1) * EDGE)
        s[span, span] = unpack_diagonal(got[r * GROUPS + r, at:at + HELD])


def first_kernel(got, lower, inverse, s, a, w):
    unpack(got, 0, s)
    factor_panel(s, lower, inverse, a, w)


def second_kernel(got, inverse0, across, lower, inverse, s, a, w):
    for r in range(GROUPS):
        for c in range(GROUPS):
            s[r * EDGE:(r + 1) * EDGE, c * EDGE:(c + 1) * EDGE] = got[r * GROUPS + c, :EDGE]
    across[...] = dot3(split2(s[...]), split2(inverse0[...]), NT)
    unpack(got, EDGE, s)
    part = split2(across[...])
    s[...] = s[...] - dot3(part, part, NT)
    factor_panel(s, lower, inverse, a, w)


def collect(ids, at, flags):
    for number, flag in flags:
        ids[at] = number
        at = at + jnp.where(flag, 1, 0)
    return at


def visit(ids, first, last, product, target):
    def step(i, _):
        slots = [first + i * BATCH + j for j in range(BATCH)]
        numbers = [ids[jnp.minimum(slot, last - 1)] for slot in slots]
        changes = [jnp.where(slot < last, product(number), 0.0) for slot, number in zip(slots, numbers)]
        for number, change in zip(numbers, changes):
            target(number, change)
        return 0

    lax.fori_loop(0, lax.div(last - first + BATCH - 1, BATCH), step, 0)


def spans(i):
    return pl.ds(pl.multiple_of(i * EDGE, EDGE), EDGE)


def last_kernel(front, pattern, ar, ac0, ac1, ac3, ac2, low0, inv0, across, low1, inv1, out,
                buf, arv, acv, xh, xl, yh, yl, th, tl, sh, sl, bh, bl, lr, lc, ids, arrive, leave):
    r, c = lax.axis_index("row"), lax.axis_index("col")
    own, mine = spans(c), spans(r)
    half = WIDTH // 2
    loads = []
    for k in range(NPAN):
        loads.append(pltpu.make_async_copy(ar.at[:, k], arv.at[:, k], arrive.at[8 * k]))
        for s, ac in ((0, ac0), (1, ac1), (2, ac2), (3, ac3)):
            loads.append(pltpu.make_async_copy(ac.at[k], acv.at[(r + GROUPS - s) % GROUPS, k], arrive.at[8 * k + s + 1]))
    fronts = [pltpu.make_async_copy(front.at[l], buf.at[l], arrive.at[16 + l]) for l in range(NPAN, LB)]
    for load in loads + fronts:
        load.start()
    zero = jnp.zeros((EDGE, EDGE), F32)
    for l in range(NPAN):
        for m in range(NPAN, LB):
            buf[l, :, m, :] = zero
    buf[0, :, 1, :] = zero
    buf[0, :, 0, :] = low0[mine, own]
    buf[1, :, 0, :] = across[mine, own]
    buf[1, :, 1, :] = low1[mine, own]
    stores = [pltpu.make_async_copy(buf.at[:NPAN], out.at[:NPAN], leave.at[0])]
    stores[0].start()
    bh[...], bl[...] = split2(across[...])
    side = [(l, g) for l in range(REST) for g in range(GROUPS)]
    row_end = collect(ids, 0, [
        (l * TILE + g, pattern[0, (l + NPAN) * GROUPS + r, GROUPS + g] > 0) for l, g in side])
    col_end = collect(ids, row_end, [
        (l * TILE + g, pattern[0, GROUPS + g, (l + NPAN) * GROUPS + c] > 0) for l, g in side])
    all_end = collect(ids, col_end, [
        ((k * TILE + l) * TILE + m, pattern[k, (l + NPAN) * GROUPS + r, (m + NPAN) * GROUPS + c] > 0)
        for k in range(NPAN) for l in range(REST) for m in range(REST)])

    def row_product(number):
        l, g = lax.div(number, TILE), lax.rem(number, TILE)
        return dot3((xh[0, spans(l), :], xl[0, spans(l), :]), (bh[spans(g), :], bl[spans(g), :]), NT)

    def row_target(number, change):
        l, g = lax.div(number, TILE), lax.rem(number, TILE)
        arv[g, 1, l] = arv[g, 1, l] - change

    def col_product(number):
        l, g = lax.div(number, TILE), lax.rem(number, TILE)
        return dot3((bh[spans(g), :], bl[spans(g), :]), (yh[0, :, spans(l)], yl[0, :, spans(l)]), NN)

    def col_target(number, change):
        l, g = lax.div(number, TILE), lax.rem(number, TILE)
        acv[g, 1, :, spans(l)] = acv[g, 1, :, spans(l)] - change

    def place(number):
        row = lax.div(number, TILE)
        return lax.div(row, TILE), lax.rem(row, TILE), lax.rem(number, TILE)

    def product(number):
        k, l, m = place(number)
        return dot3((xh[k, spans(l), :], xl[k, spans(l), :]), (yh[k, :, spans(m)], yl[k, :, spans(m)]), NN)

    def target(number, change):
        k, l, m = place(number)
        buf[l + NPAN, :, m + NPAN, :] = buf[l + NPAN, :, m + NPAN, :] - change

    for k in range(NPAN):
        for load in loads[5 * k:5 * k + 5]:
            load.wait()
        if k == 1:
            visit(ids, 0, row_end, row_product, row_target)
            visit(ids, row_end, col_end, col_product, col_target)
        for g in range(GROUPS):
            span = slice(g * EDGE, (g + 1) * EDGE)
            th[:, span], tl[:, span] = split2(arv[g, k].reshape(ROWS, EDGE))
            sh[span, :], sl[span, :] = split2(acv[g, k])
        wh, wl = split2((inv0, inv1)[k][...])
        lr[:, :half] = dot3((th[:, :half], tl[:, :half]), (wh[:half, :half], wl[:half, :half]), NT)
        lr[:, half:] = dot3((th[...], tl[...]), (wh[half:, :], wl[half:, :]), NT)
        xh[k], xl[k] = split2(lr[...])
        lc[:half, :] = dot3((wh[:half, :half], wl[:half, :half]), (sh[:half, :], sl[:half, :]), NN)
        lc[half:, :] = dot3((wh[half:, :], wl[half:, :]), (sh[...], sl[...]), NN)
        yh[k], yl[k] = split2(lc[...])
        if k == 0:
            for load in fronts:
                load.wait()
        for l in range(REST):
            buf[l + NPAN, :, k, :] = lr[l * EDGE:(l + 1) * EDGE, own]
    visit(ids, col_end, all_end, product, target)
    stores.append(pltpu.make_async_copy(buf.at[NPAN:], out.at[NPAN:], leave.at[1]))
    stores[-1].start()
    for store in stores:
        store.wait()


def run(copies):
    for copy in copies:
        copy.start()
    for copy in copies:
        copy.wait()


def extract_kernel(front, ar, ac, rows, cols, sem):
    copy = pltpu.make_async_copy
    loads = [copy(front.at[NPAN:, :, k, :], rows.at[k], sem.at[k]) for k in range(NPAN)]
    for k in range(NPAN):
        for j in range(REST):
            loads.append(copy(front.at[k, :, j + NPAN, :], cols.at[k, :, j * EDGE:(j + 1) * EDGE], sem.at[len(loads)]))
    run(loads)
    run([copy(rows, ar, sem.at[0]), copy(cols, ac, sem.at[1])])


def corner_kernel(front, c0, c1, first, second, third, send0, send1, sem):
    r, c = lax.axis_index("row"), lax.axis_index("col")
    copy = pltpu.make_async_copy
    every = GROUPS * GROUPS
    loads = [copy(front.at[l, :, m, :], to, sem.at[i])
             for i, (l, m, to) in enumerate(((0, 0, first), (1, 0, send1.at[:EDGE]), (1, 1, third)))]
    for one in loads:
        one.start()
    loads[0].wait()
    pack(first[...], send0, r, c)
    stores = [copy(send0, c0.at[g], sem.at[3 + g]) for g in range(every)]
    for one in stores:
        one.start()
    loads[1].wait()
    loads[2].wait()
    pack(third[...], second, r, c)
    send1[EDGE:, :] = second[...]
    last = [copy(send1, c1.at[g], sem.at[3 + every + g]) for g in range(every)]
    for one in last:
        one.start()
    for one in stores + last:
        one.wait()


def shape(*dims):
    return jax.ShapeDtypeStruct(dims, F32)


def vmem(*dims, dtype=F32):
    return pltpu.VMEM(dims, dtype)


def call(kernel, outs, scratch=(), limit=60, **kw):
    return pl.pallas_call(
        kernel, out_shape=outs, scratch_shapes=list(scratch),
        compiler_params=pltpu.CompilerParams(vmem_limit_bytes=limit * 1024 * 1024), **kw)


def per_device(front, pattern):
    blocks = front[0, :, :, 0]
    work = [vmem(WIDTH, WIDTH), vmem(GROUPS, EDGE, EDGE), vmem(GROUPS, EDGE, EDGE)]
    square = shape(WIDTH, WIDTH)
    every = GROUPS * GROUPS
    away, dma = pl.BlockSpec(memory_space=pltpu.HBM), pltpu.SemaphoreType.DMA
    c0, c1 = call(
        corner_kernel, [shape(every, HELD, EDGE), shape(every, EDGE + HELD, EDGE)],
        [vmem(EDGE, EDGE), vmem(HELD, EDGE), vmem(EDGE, EDGE), vmem(HELD, EDGE), vmem(EDGE + HELD, EDGE), dma((3 + 2 * every,))],
        in_specs=[away], out_specs=[away, away],
    )(blocks)
    later, c0 = lax.optimization_barrier((blocks, c0))
    got0 = lax.all_to_all(c0, ("row", "col"), 0, 0, tiled=True)
    ar, ac = call(
        extract_kernel, [shape(NPAN, REST, EDGE, EDGE), shape(NPAN, EDGE, ROWS)],
        [vmem(NPAN, REST, EDGE, EDGE), vmem(NPAN, EDGE, ROWS), dma((NPAN + NPAN * REST,))],
        in_specs=[away], out_specs=[away, away],
    )(later)
    ar = lax.all_gather(ar, "col", axis=0)
    c1, got0 = lax.optimization_barrier((c1, got0))
    got1 = lax.all_to_all(c1, ("row", "col"), 0, 0, tiled=True)
    low0, inv0 = call(first_kernel, [square] * 2, work)(got0)
    ac, got1, inv0 = lax.optimization_barrier((ac, got1, inv0))
    acs = [ac] + [lax.ppermute(ac, "row", [(i, (i + s) % GROUPS) for i in range(GROUPS)]) for s in (1, 3, 2)]
    across, low1, inv1 = call(second_kernel, [square] * 3, work)(got1, inv0)
    whole = pl.BlockSpec(memory_space=pltpu.VMEM)
    result = call(
        last_kernel, shape(LB, EDGE, LB, EDGE),
        [vmem(LB, EDGE, LB, EDGE), vmem(GROUPS, NPAN, REST, EDGE, EDGE), vmem(GROUPS, NPAN, EDGE, ROWS)]
        + [vmem(NPAN, ROWS, WIDTH, dtype=BF16)] * 2 + [vmem(NPAN, WIDTH, ROWS, dtype=BF16)] * 2 + [vmem(ROWS, WIDTH, dtype=BF16)] * 2
        + [vmem(WIDTH, ROWS, dtype=BF16)] * 2 + [vmem(WIDTH, WIDTH, dtype=BF16)] * 2
        + [vmem(ROWS, WIDTH), vmem(WIDTH, ROWS), pltpu.SMEM((128,), jnp.int32), dma((24,)), dma((2,))],
        in_specs=[away, pl.BlockSpec(memory_space=pltpu.SMEM), away, away, away, away, away] + [whole] * 5,
        out_specs=away,
    )(blocks, pattern, ar, *acs, low0, inv0, across, low1, inv1)
    return result[None, :, :, None]


def solution(mesh):
    placed = (P("row", "front", None, "col", None, None), P("front", None, None))
    return jax.shard_map(
        per_device, mesh=mesh, in_specs=placed,
        out_specs=P("row", "front", None, "col", None, None), check_vma=False,
    )
```

```python
import functools

import jax
import jax.numpy as jnp
from jax import lax
from jax.experimental import pallas as pl
from jax.experimental.pallas import tpu as pltpu
from jax.sharding import PartitionSpec as P

F32 = jnp.float32
BF16 = jnp.bfloat16
HI = lax.Precision.HIGHEST
EDGE = 128
TILE = 8
HALF = EDGE // 2
HELD = HALF + TILE
GROUPS = 4
WIDTH = EDGE * GROUPS
LB = 8
BATCH = 4
NPAN = 2
REST = LB - NPAN
ROWS = REST * EDGE

NN = (((1,), (0,)), ((), ()))
NT = (((1,), (1,)), ((), ()))
TN = (((0,), (0,)), ((), ()))


def exact_dot(a, b, dims):
    return lax.dot_general(a, b, dims, precision=HI, preferred_element_type=F32)


def split2(x):
    high = x.astype(BF16)
    return high, (x - high.astype(F32)).astype(BF16)


def split3(x):
    high = x.astype(BF16)
    rest = x - high.astype(F32)
    mid = rest.astype(BF16)
    return high, mid, (rest - mid.astype(F32)).astype(BF16)


def dot3(a, b, dims):
    one = functools.partial(lax.dot_general, dimension_numbers=dims, preferred_element_type=F32)
    return one(a[0], b[0]) + (one(a[0], b[1]) + one(a[1], b[0]))


def spread(x):
    return jnp.broadcast_to(x, (TILE, EDGE))


def factor_block(a, w):
    sub = lax.broadcasted_iota(jnp.int32, (TILE, EDGE), 0)
    count = EDGE // TILE

    def tile(p):
        return slice(TILE * p, TILE * (p + 1))

    def columns(x, p):
        return [spread(x[:, TILE * p + q:TILE * p + q + 1]) for q in range(TILE)]

    rows = [(a[tile(p), :], w[tile(p), :]) for p in range(2)]
    cols = columns(rows[0][0], 0)
    for p in range(count):
        if p + 2 < count:
            rows.append((a[tile(p + 2), :], w[tile(p + 2), :]))
        below = [columns(left, p) for left, _ in rows[1:]]
        corner = columns(rows[1][0], p + 1) if len(rows) > 1 else None
        invs = jnp.zeros((TILE, EDGE), F32)
        pivot = spread(cols[0][:1, :])
        for q in range(TILE):
            inv = 1.0 / pivot
            if q + 1 < TILE:
                beside = spread(cols[q + 1][q:q + 1, :])
                pivot = spread(cols[q + 1][q + 1:q + 2, :]) - (beside * beside) * inv
            invs = jnp.where(sub == q, inv, invs)
            factors = [jnp.where(sub > q, cols[q], 0.0) * inv] + [one[q] * inv for one in below]
            left, right = (spread(x[q:q + 1, :]) for x in rows[0])
            rows = [(x - m * left, y - m * right) for (x, y), m in zip(rows, factors)]
            if corner is not None:
                corner = [x - factors[1] * spread(below[0][q][t:t + 1, :]) for t, x in enumerate(corner)]
            for t in range(q + 1, TILE):
                across = spread(cols[t][q:q + 1, :])
                for one, m in zip([cols] + below, factors):
                    one[t] = one[t] - m * across
        root = lax.rsqrt(invs) * invs
        left, right = rows[0][0] * root, rows[0][1] * root
        a[tile(p), :], w[tile(p), :] = left, right
        low = TILE * (p + 3)
        if low < EDGE:
            h, m, l = split3(left)
            vh, vm, vl = split3(right)
            uh, um, ul = (jnp.concatenate(pair, 1) for pair in ((h, vh), (m, vm), (l, vl)))
            lhs = jnp.concatenate([h, h, m, h, m, l], 0)
            rhs = jnp.concatenate([uh, um, uh, ul, um, uh], 0)
            change = lax.dot_general(lhs, rhs, TN, preferred_element_type=F32)
            a[low:, :] = a[low:, :] - change[low:, :EDGE]
            w[low:, :] = w[low:, :] - change[low:, EDGE:]
        rows, cols = rows[1:], corner


def factor_panel(s, lower, inverse, a, w, low_out, inv_out, sem):
    ri = lax.broadcasted_iota(jnp.int32, (EDGE, EDGE), 0)
    ci = lax.broadcasted_iota(jnp.int32, (EDGE, EDGE), 1)
    copies = []
    for k in range(GROUPS):
        here = slice(k * EDGE, (k + 1) * EDGE)
        below = slice((k + 1) * EDGE, WIDTH)
        before = slice(0, k * EDGE)
        if k + 1 < GROUPS:
            lower[here, below] = jnp.zeros((EDGE, WIDTH - (k + 1) * EDGE), F32)
            inverse[here, below] = jnp.zeros((EDGE, WIDTH - (k + 1) * EDGE), F32)
        a[k] = s[here, here]
        w[k] = jnp.where(ri == ci, 1.0, 0.0)
        factor_block(a.at[k], w.at[k])
        d = w[k]
        if k + 1 < GROUPS:
            part = exact_dot(s[below, here], d, NT)
            lower[below, here] = part
            s[below, below] = s[below, below] - exact_dot(part, part, NT)
        lower[here, here] = jnp.where(ri <= ci, a[k], 0.0).T
        inverse[here, here] = d
        if k > 0:
            part = exact_dot(lower[here, before], inverse[before, before], NN)
            inverse[here, before] = -exact_dot(d, part, NN)
        for i, (held, to) in enumerate(((lower, low_out), (inverse, inv_out))):
            copies.append(pltpu.make_async_copy(held.at[here], to.at[here], sem.at[2 * k + i]))
            copies[-1].start()
    for copy in copies:
        copy.wait()


def pack(block, ref, r, c):
    row = lax.broadcasted_iota(jnp.int32, (HALF, EDGE), 0)
    lane = lax.broadcasted_iota(jnp.int32, (HALF, EDGE), 1)
    top, low = block[:HALF], block[HALF:]
    diagonal = jnp.where(lane - HALF > row, pltpu.roll(top, HALF, 1), low)
    ref[:HALF, :] = jnp.where(r == c, diagonal, jnp.where(r > c, top, block.T[HALF:]))
    ref[HALF:HELD, :] = spread(jnp.sum(jnp.where(lane == row, top, 0.0), axis=0, keepdims=True))


def unpack_diagonal(got):
    row = lax.broadcasted_iota(jnp.int32, (EDGE, EDGE), 0)
    lane = lax.broadcasted_iota(jnp.int32, (EDGE, EDGE), 1)
    body = got[:HALF]
    some = jnp.concatenate([pltpu.roll(body, HALF, 1), body], 0)
    kept = ((row >= HALF) & (lane <= row)) | ((lane < HALF) & (row < lane))
    whole = jnp.where(kept, some, some.T)
    return jnp.where((row == lane) & (row < HALF), jnp.broadcast_to(got[HALF:HALF + 1], (EDGE, EDGE)), whole)


def unpack(got, s):
    for r in range(GROUPS):
        for c in range(r):
            span = slice(c * EDGE, (c + 1) * EDGE)
            s[r * EDGE:r * EDGE + HALF, span] = got[r * GROUPS + c, 0:HALF]
            s[r * EDGE + HALF:(r + 1) * EDGE, span] = got[c * GROUPS + r, 0:HALF]
        span = slice(r * EDGE, (r + 1) * EDGE)
        s[span, span] = unpack_diagonal(got[r * GROUPS + r, 0:HELD])


def first_kernel(got, low_out, inv_out, s, lower, inverse, a, w, sem):
    unpack(got, s)
    factor_panel(s, lower, inverse, a, w, low_out, inv_out, sem)


def second_kernel(got, inverse0, across_out, low_out, inv_out, s, lower, inverse, a, w, sem, rect, square, across, invs, sem2):
    loads = [pltpu.make_async_copy(*pair, sem2.at[i]) for i, pair in enumerate(
        ((inverse0, invs), (got.at[:, :EDGE], rect), (got.at[:, EDGE:], square)))]
    for load in loads:
        load.start()
    loads[0].wait()
    inv = split2(invs[...])
    loads[1].wait()
    for r in range(GROUPS):
        for c in range(GROUPS):
            s[r * EDGE:(r + 1) * EDGE, c * EDGE:(c + 1) * EDGE] = rect[r * GROUPS + c]
    across[...] = dot3(split2(s[...]), inv, NT)
    store = pltpu.make_async_copy(across, across_out, sem2.at[3])
    store.start()
    loads[2].wait()
    unpack(square, s)
    part = split2(across[...])
    s[...] = s[...] - dot3(part, part, NT)
    factor_panel(s, lower, inverse, a, w, low_out, inv_out, sem)
    store.wait()


def collect(ids, at, flags):
    for number, flag in flags:
        ids[at] = number
        at = at + jnp.where(flag, 1, 0)
    return at


def visit(ids, first, last, product, target):
    def step(i, _):
        slots = [first + i * BATCH + j for j in range(BATCH)]
        numbers = [ids[jnp.minimum(slot, last - 1)] for slot in slots]
        changes = [jnp.where(slot < last, product(number), 0.0) for slot, number in zip(slots, numbers)]
        for number, change in zip(numbers, changes):
            target(number, change)
        return 0

    lax.fori_loop(0, lax.div(last - first + BATCH - 1, BATCH), step, 0)


def spans(i):
    return pl.ds(pl.multiple_of(i * EDGE, EDGE), EDGE)


def last_kernel(front, pattern, ar, ac0, ac1, ac3, ac2, low0, inv0, across, low1, inv1, out,
                buf, arv, acv, xh, xl, yh, yl, th, tl, sh, sl, bh, bl, lr, lc, ids, arrive, leave):
    r, c = lax.axis_index("row"), lax.axis_index("col")
    own, mine = spans(c), spans(r)
    half = WIDTH // 2
    loads = []
    for k in range(NPAN):
        loads.append(pltpu.make_async_copy(ar.at[:, k], arv.at[:, k], arrive.at[8 * k]))
        for s, ac in ((0, ac0), (1, ac1), (2, ac2), (3, ac3)):
            loads.append(pltpu.make_async_copy(ac.at[k], acv.at[(r + GROUPS - s) % GROUPS, k], arrive.at[8 * k + s + 1]))
    fronts = [pltpu.make_async_copy(front.at[l], buf.at[l], arrive.at[16 + l]) for l in range(NPAN, LB)]
    for load in loads + fronts:
        load.start()
    zero = jnp.zeros((EDGE, EDGE), F32)
    for l in range(NPAN):
        for m in range(NPAN, LB):
            buf[l, :, m, :] = zero
    buf[0, :, 1, :] = zero
    buf[0, :, 0, :] = low0[mine, own]
    buf[1, :, 0, :] = across[mine, own]
    buf[1, :, 1, :] = low1[mine, own]
    store = pltpu.make_async_copy(buf.at[:NPAN], out.at[:NPAN], leave.at[0])
    store.start()
    bh[...], bl[...] = split2(across[...])
    side = [(l, g) for l in range(REST) for g in range(GROUPS)]
    row_end = collect(ids, 0, [
        (l * TILE + g, pattern[0, (l + NPAN) * GROUPS + r, GROUPS + g] > 0) for l, g in side])
    col_end = collect(ids, row_end, [
        (l * TILE + g, pattern[0, GROUPS + g, (l + NPAN) * GROUPS + c] > 0) for l, g in side])
    all_end = collect(ids, col_end, [
        ((k * TILE + l) * TILE + m, pattern[k, (l + NPAN) * GROUPS + r, (m + NPAN) * GROUPS + c] > 0)
        for k in range(NPAN) for l in range(REST) for m in range(REST)])

    def row_product(number):
        l, g = lax.div(number, TILE), lax.rem(number, TILE)
        return dot3((xh[0, spans(l), :], xl[0, spans(l), :]), (bh[spans(g), :], bl[spans(g), :]), NT)

    def row_target(number, change):
        l, g = lax.div(number, TILE), lax.rem(number, TILE)
        arv[g, 1, l] = arv[g, 1, l] - change

    def col_product(number):
        l, g = lax.div(number, TILE), lax.rem(number, TILE)
        return dot3((bh[spans(g), :], bl[spans(g), :]), (yh[0, :, spans(l)], yl[0, :, spans(l)]), NN)

    def col_target(number, change):
        l, g = lax.div(number, TILE), lax.rem(number, TILE)
        acv[g, 1, :, spans(l)] = acv[g, 1, :, spans(l)] - change

    def place(number):
        row = lax.div(number, TILE)
        return lax.div(row, TILE), lax.rem(row, TILE), lax.rem(number, TILE)

    def product(number):
        k, l, m = place(number)
        return dot3((xh[k, spans(l), :], xl[k, spans(l), :]), (yh[k, :, spans(m)], yl[k, :, spans(m)]), NN)

    def target(number, change):
        k, l, m = place(number)
        buf[l + NPAN, :, m + NPAN, :] = buf[l + NPAN, :, m + NPAN, :] - change

    for k in range(NPAN):
        for load in loads[5 * k:5 * k + 5]:
            load.wait()
        if k == 1:
            visit(ids, 0, row_end, row_product, row_target)
            visit(ids, row_end, col_end, col_product, col_target)
        for g in range(GROUPS):
            span = slice(g * EDGE, (g + 1) * EDGE)
            th[:, span], tl[:, span] = split2(arv[g, k].reshape(ROWS, EDGE))
            sh[span, :], sl[span, :] = split2(acv[g, k])
        wh, wl = split2((inv0, inv1)[k][...])
        lr[:, :half] = dot3((th[:, :half], tl[:, :half]), (wh[:half, :half], wl[:half, :half]), NT)
        lr[:, half:] = dot3((th[...], tl[...]), (wh[half:, :], wl[half:, :]), NT)
        xh[k], xl[k] = split2(lr[...])
        lc[:half, :] = dot3((wh[:half, :half], wl[:half, :half]), (sh[:half, :], sl[:half, :]), NN)
        lc[half:, :] = dot3((wh[half:, :], wl[half:, :]), (sh[...], sl[...]), NN)
        yh[k], yl[k] = split2(lc[...])
        if k == 0:
            for load in fronts:
                load.wait()
        for l in range(REST):
            buf[l + NPAN, :, k, :] = lr[l * EDGE:(l + 1) * EDGE, own]
    visit(ids, col_end, all_end, product, target)
    last = pltpu.make_async_copy(buf.at[NPAN:], out.at[NPAN:], leave.at[1])
    last.start()
    store.wait()
    last.wait()


def run(copies):
    for copy in copies:
        copy.start()
    for copy in copies:
        copy.wait()


def extract_kernel(front, ar, ac, rows, cols, sem):
    copy = pltpu.make_async_copy
    loads = [copy(front.at[NPAN:, :, k, :], rows.at[k], sem.at[k]) for k in range(NPAN)]
    for k in range(NPAN):
        for j in range(REST):
            loads.append(copy(front.at[k, :, j + NPAN, :], cols.at[k, :, j * EDGE:(j + 1) * EDGE], sem.at[len(loads)]))
    run(loads)
    run([copy(rows, ar, sem.at[0]), copy(cols, ac, sem.at[1])])


def corner_kernel(front, c0, c1, first, second, third, send0, send1, sem):
    r, c = lax.axis_index("row"), lax.axis_index("col")
    copy = pltpu.make_async_copy
    every = GROUPS * GROUPS
    loads = [copy(front.at[l, :, m, :], to, sem.at[i])
             for i, (l, m, to) in enumerate(((0, 0, first), (1, 0, send1.at[:EDGE]), (1, 1, third)))]
    for one in loads:
        one.start()
    loads[0].wait()
    pack(first[...], send0, r, c)
    stores = [copy(send0, c0.at[g], sem.at[3 + g]) for g in range(every)]
    for one in stores:
        one.start()
    loads[1].wait()
    loads[2].wait()
    pack(third[...], second, r, c)
    send1[EDGE:, :] = second[...]
    last = [copy(send1, c1.at[g], sem.at[3 + every + g]) for g in range(every)]
    for one in last:
        one.start()
    for one in stores + last:
        one.wait()


def shape(*dims):
    return jax.ShapeDtypeStruct(dims, F32)


def vmem(*dims, dtype=F32):
    return pltpu.VMEM(dims, dtype)


def call(kernel, outs, scratch=(), limit=60, **kw):
    return pl.pallas_call(
        kernel, out_shape=outs, scratch_shapes=list(scratch),
        compiler_params=pltpu.CompilerParams(vmem_limit_bytes=limit * 1024 * 1024), **kw)


def per_device(front, pattern):
    blocks = front[0, :, :, 0]
    square = shape(WIDTH, WIDTH)
    every = GROUPS * GROUPS
    away, dma = pl.BlockSpec(memory_space=pltpu.HBM), pltpu.SemaphoreType.DMA
    work = [vmem(WIDTH, WIDTH)] * 3 + [vmem(GROUPS, EDGE, EDGE)] * 2 + [dma((LB,))]
    c0, c1 = call(
        corner_kernel, [shape(every, HELD, EDGE), shape(every, EDGE + HELD, EDGE)],
        [vmem(EDGE, EDGE), vmem(HELD, EDGE), vmem(EDGE, EDGE), vmem(HELD, EDGE), vmem(EDGE + HELD, EDGE), dma((3 + 2 * every,))],
        in_specs=[away], out_specs=[away, away],
    )(blocks)
    later, c0 = lax.optimization_barrier((blocks, c0))
    got0 = lax.all_to_all(c0, ("row", "col"), 0, 0, tiled=True)
    ar, ac = call(
        extract_kernel, [shape(NPAN, REST, EDGE, EDGE), shape(NPAN, EDGE, ROWS)],
        [vmem(NPAN, REST, EDGE, EDGE), vmem(NPAN, EDGE, ROWS), dma((NPAN + NPAN * REST,))],
        in_specs=[away], out_specs=[away, away],
    )(later)
    ar = lax.all_gather(ar, "col", axis=0)
    c1, ac, got0 = lax.optimization_barrier((c1, ac, got0))
    got1 = lax.all_to_all(c1, ("row", "col"), 0, 0, tiled=True)
    low0, inv0 = call(first_kernel, [square] * 2, work, out_specs=[away] * 2)(got0)
    later, inv0 = lax.optimization_barrier((ac, inv0))
    acs = [ac] + [lax.ppermute(piece, "row", [(i, (i + s) % GROUPS) for i in range(GROUPS)])
                  for s, piece in ((1, later), (3, later), (2, ac))]
    across, low1, inv1 = call(
        second_kernel, [square] * 3,
        work + [vmem(every, EDGE, EDGE), vmem(every, HELD, EDGE), vmem(WIDTH, WIDTH), vmem(WIDTH, WIDTH), dma((4,))],
        in_specs=[away] * 2, out_specs=[away] * 3,
    )(got1, inv0)
    whole = pl.BlockSpec(memory_space=pltpu.VMEM)
    result = call(
        last_kernel, shape(LB, EDGE, LB, EDGE),
        [vmem(LB, EDGE, LB, EDGE), vmem(GROUPS, NPAN, REST, EDGE, EDGE), vmem(GROUPS, NPAN, EDGE, ROWS)]
        + [vmem(NPAN, ROWS, WIDTH, dtype=BF16)] * 2 + [vmem(NPAN, WIDTH, ROWS, dtype=BF16)] * 2 + [vmem(ROWS, WIDTH, dtype=BF16)] * 2
        + [vmem(WIDTH, ROWS, dtype=BF16)] * 2 + [vmem(WIDTH, WIDTH, dtype=BF16)] * 2
        + [vmem(ROWS, WIDTH), vmem(WIDTH, ROWS), pltpu.SMEM((128,), jnp.int32), dma((24,)), dma((2,))],
        in_specs=[away, pl.BlockSpec(memory_space=pltpu.SMEM), away, away, away, away, away] + [whole] * 5,
        out_specs=away,
    )(blocks, pattern, ar, *acs, low0, inv0, across, low1, inv1)
    return result[None, :, :, None]


def solution(mesh):
    placed = (P("row", "front", None, "col", None, None), P("front", None, None))
    return jax.shard_map(
        per_device, mesh=mesh, in_specs=placed,
        out_specs=P("row", "front", None, "col", None, None), check_vma=False,
    )
```

```python
import functools

import jax
import jax.numpy as jnp
from jax import lax
from jax.experimental import pallas as pl
from jax.experimental.pallas import tpu as pltpu
from jax.sharding import PartitionSpec as P

F32 = jnp.float32
BF16 = jnp.bfloat16
HI = lax.Precision.HIGHEST
EDGE = 128
TILE = 8
HALF = EDGE // 2
HELD = HALF + TILE
GROUPS = 4
WIDTH = EDGE * GROUPS
LB = 8
BATCH = 4
NPAN = 2
REST = LB - NPAN
ROWS = REST * EDGE

NN = (((1,), (0,)), ((), ()))
NT = (((1,), (1,)), ((), ()))
TN = (((0,), (0,)), ((), ()))


def exact_dot(a, b, dims):
    return lax.dot_general(a, b, dims, precision=HI, preferred_element_type=F32)


def split2(x):
    high = x.astype(BF16)
    return high, (x - high.astype(F32)).astype(BF16)


def split3(x):
    high = x.astype(BF16)
    rest = x - high.astype(F32)
    mid = rest.astype(BF16)
    return high, mid, (rest - mid.astype(F32)).astype(BF16)


def dot3(a, b, dims):
    one = functools.partial(lax.dot_general, dimension_numbers=dims, preferred_element_type=F32)
    return one(a[0], b[0]) + (one(a[0], b[1]) + one(a[1], b[0]))


def spread(x):
    return jnp.broadcast_to(x, (TILE, EDGE))


def factor_block(a, w):
    sub = lax.broadcasted_iota(jnp.int32, (TILE, EDGE), 0)
    count = EDGE // TILE

    def tile(p):
        return slice(TILE * p, TILE * (p + 1))

    def columns(x, p):
        return [spread(x[:, TILE * p + q:TILE * p + q + 1]) for q in range(TILE)]

    rows = [(a[tile(p), :], w[tile(p), :]) for p in range(2)]
    cols = columns(rows[0][0], 0)
    for p in range(count):
        if p + 2 < count:
            rows.append((a[tile(p + 2), :], w[tile(p + 2), :]))
        below = [columns(left, p) for left, _ in rows[1:]]
        corner = columns(rows[1][0], p + 1) if len(rows) > 1 else None
        invs = jnp.zeros((TILE, EDGE), F32)
        pivot = spread(cols[0][:1, :])
        for q in range(TILE):
            inv = 1.0 / pivot
            if q + 1 < TILE:
                beside = spread(cols[q + 1][q:q + 1, :])
                pivot = spread(cols[q + 1][q + 1:q + 2, :]) - (beside * beside) * inv
            invs = jnp.where(sub == q, inv, invs)
            factors = [jnp.where(sub > q, cols[q], 0.0) * inv] + [one[q] * inv for one in below]
            left, right = (spread(x[q:q + 1, :]) for x in rows[0])
            rows = [(x - m * left, y - m * right) for (x, y), m in zip(rows, factors)]
            if corner is not None:
                corner = [x - factors[1] * spread(below[0][q][t:t + 1, :]) for t, x in enumerate(corner)]
            for t in range(q + 1, TILE):
                across = spread(cols[t][q:q + 1, :])
                for one, m in zip([cols] + below, factors):
                    one[t] = one[t] - m * across
        root = lax.rsqrt(invs) * invs
        left, right = rows[0][0] * root, rows[0][1] * root
        a[tile(p), :], w[tile(p), :] = left, right
        low = TILE * (p + 3)
        if low < EDGE:
            h, m, l = split3(left)
            vh, vm, vl = split3(right)
            uh, um, ul = (jnp.concatenate(pair, 1) for pair in ((h, vh), (m, vm), (l, vl)))
            lhs = jnp.concatenate([h, h, m, h, m, l], 0)
            rhs = jnp.concatenate([uh, um, uh, ul, um, uh], 0)
            change = lax.dot_general(lhs, rhs, TN, preferred_element_type=F32)
            a[low:, :] = a[low:, :] - change[low:, :EDGE]
            w[low:, :] = w[low:, :] - change[low:, EDGE:]
        rows, cols = rows[1:], corner


def factor_panel(s, lower, inverse, a, w, low_out, inv_out, sem):
    ri = lax.broadcasted_iota(jnp.int32, (EDGE, EDGE), 0)
    ci = lax.broadcasted_iota(jnp.int32, (EDGE, EDGE), 1)
    copies = []
    for k in range(GROUPS):
        here = slice(k * EDGE, (k + 1) * EDGE)
        below = slice((k + 1) * EDGE, WIDTH)
        before = slice(0, k * EDGE)
        if k + 1 < GROUPS:
            lower[here, below] = jnp.zeros((EDGE, WIDTH - (k + 1) * EDGE), F32)
            inverse[here, below] = jnp.zeros((EDGE, WIDTH - (k + 1) * EDGE), F32)
        a[k] = s[here, here]
        w[k] = jnp.where(ri == ci, 1.0, 0.0)
        factor_block(a.at[k], w.at[k])
        d = w[k]
        if k + 1 < GROUPS:
            part = exact_dot(s[below, here], d, NT)
            lower[below, here] = part
            s[below, below] = s[below, below] - exact_dot(part, part, NT)
        lower[here, here] = jnp.where(ri <= ci, a[k], 0.0).T
        inverse[here, here] = d
        if k > 0:
            part = exact_dot(lower[here, before], inverse[before, before], NN)
            inverse[here, before] = -exact_dot(d, part, NN)
        for i, (held, to) in enumerate(((lower, low_out), (inverse, inv_out))):
            copies.append(pltpu.make_async_copy(held.at[here], to.at[here], sem.at[2 * k + i]))
            copies[-1].start()
    for copy in copies:
        copy.wait()


def pack(block, ref, r, c):
    row = lax.broadcasted_iota(jnp.int32, (HALF, EDGE), 0)
    lane = lax.broadcasted_iota(jnp.int32, (HALF, EDGE), 1)
    top, low = block[:HALF], block[HALF:]
    diagonal = jnp.where(lane - HALF > row, pltpu.roll(top, HALF, 1), low)
    ref[:HALF, :] = jnp.where(r == c, diagonal, jnp.where(r > c, top, block.T[HALF:]))
    ref[HALF:HELD, :] = spread(jnp.sum(jnp.where(lane == row, top, 0.0), axis=0, keepdims=True))


def unpack_diagonal(got):
    row = lax.broadcasted_iota(jnp.int32, (EDGE, EDGE), 0)
    lane = lax.broadcasted_iota(jnp.int32, (EDGE, EDGE), 1)
    body = got[:HALF]
    some = jnp.concatenate([pltpu.roll(body, HALF, 1), body], 0)
    kept = ((row >= HALF) & (lane <= row)) | ((lane < HALF) & (row < lane))
    whole = jnp.where(kept, some, some.T)
    return jnp.where((row == lane) & (row < HALF), jnp.broadcast_to(got[HALF:HALF + 1], (EDGE, EDGE)), whole)


def unpack(got, s):
    for r in range(GROUPS):
        for c in range(r):
            span = slice(c * EDGE, (c + 1) * EDGE)
            s[r * EDGE:r * EDGE + HALF, span] = got[r * GROUPS + c, 0:HALF]
            s[r * EDGE + HALF:(r + 1) * EDGE, span] = got[c * GROUPS + r, 0:HALF]
        span = slice(r * EDGE, (r + 1) * EDGE)
        s[span, span] = unpack_diagonal(got[r * GROUPS + r, 0:HELD])


def first_kernel(got, low_out, inv_out, s, lower, inverse, a, w, sem):
    unpack(got, s)
    factor_panel(s, lower, inverse, a, w, low_out, inv_out, sem)


def second_kernel(got, inverse0, across_out, low_out, inv_out, s, lower, inverse, a, w, sem, rect, square, across, invs, sem2):
    loads = [pltpu.make_async_copy(*pair, sem2.at[i]) for i, pair in enumerate(
        ((inverse0, invs), (got.at[:, :EDGE], rect), (got.at[:, EDGE:], square)))]
    for load in loads:
        load.start()
    loads[0].wait()
    inv = split2(invs[...])
    loads[1].wait()
    for r in range(GROUPS):
        for c in range(GROUPS):
            s[r * EDGE:(r + 1) * EDGE, c * EDGE:(c + 1) * EDGE] = rect[r * GROUPS + c]
    across[...] = dot3(split2(s[...]), inv, NT)
    store = pltpu.make_async_copy(across, across_out, sem2.at[3])
    store.start()
    loads[2].wait()
    unpack(square, s)
    part = split2(across[...])
    s[...] = s[...] - dot3(part, part, NT)
    factor_panel(s, lower, inverse, a, w, low_out, inv_out, sem)
    store.wait()


def collect(ids, at, flags):
    for number, flag in flags:
        ids[at] = number
        at = at + jnp.where(flag, 1, 0)
    return at


def visit(ids, first, last, product, target):
    def step(i, _):
        slots = [first + i * BATCH + j for j in range(BATCH)]
        numbers = [ids[jnp.minimum(slot, last - 1)] for slot in slots]
        changes = [jnp.where(slot < last, product(number), 0.0) for slot, number in zip(slots, numbers)]
        for number, change in zip(numbers, changes):
            target(number, change)
        return 0

    lax.fori_loop(0, lax.div(last - first + BATCH - 1, BATCH), step, 0)


def spans(i):
    return pl.ds(pl.multiple_of(i * EDGE, EDGE), EDGE)


def unpair(number):
    return lax.div(number, TILE), lax.rem(number, TILE)


SIDE = [(l, g) for l in range(REST) for g in range(GROUPS)]


def row_kernel(ar, pattern, inv0, across, inv1, xh_out, xl_out, mine_out,
               arv, xh, xl, th, tl, bh, bl, lr, mine, ids, arrive, leave):
    r, own = lax.axis_index("row"), spans(lax.axis_index("col"))
    half = WIDTH // 2
    loads = [pltpu.make_async_copy(ar.at[:, k], arv.at[:, k], arrive.at[k]) for k in range(NPAN)]
    for load in loads:
        load.start()
    bh[...], bl[...] = split2(across[...])
    end = collect(ids, 0, [(l * TILE + g, pattern[0, (l + NPAN) * GROUPS + r, GROUPS + g] > 0) for l, g in SIDE])

    def product(number):
        l, g = unpair(number)
        return dot3((xh[0, spans(l), :], xl[0, spans(l), :]), (bh[spans(g), :], bl[spans(g), :]), NT)

    def target(number, change):
        l, g = unpair(number)
        arv[g, 1, l] = arv[g, 1, l] - change

    stores = []
    for k in range(NPAN):
        loads[k].wait()
        if k == 1:
            visit(ids, 0, end, product, target)
        for g in range(GROUPS):
            span = slice(g * EDGE, (g + 1) * EDGE)
            th[:, span], tl[:, span] = split2(arv[g, k].reshape(ROWS, EDGE))
        wh, wl = split2((inv0, inv1)[k][...])
        lr[:, :half] = dot3((th[:, :half], tl[:, :half]), (wh[:half, :half], wl[:half, :half]), NT)
        lr[:, half:] = dot3((th[...], tl[...]), (wh[half:, :], wl[half:, :]), NT)
        xh[k], xl[k] = split2(lr[...])
        mine[k] = lr[:, own]
        for i, (held, to) in enumerate(((xh, xh_out), (xl, xl_out), (mine, mine_out))):
            stores.append(pltpu.make_async_copy(held.at[k], to.at[k], leave.at[3 * k + i]))
            stores[-1].start()
    for store in stores:
        store.wait()


def last_kernel(front, pattern, xh_in, xl_in, own_cols, ac0, ac1, ac3, ac2, low0, inv0, across, low1, inv1, out,
                buf, acv, xh, xl, yh, yl, sh, sl, bh, bl, held, lc, ids, arrive, leave):
    r, c = lax.axis_index("row"), lax.axis_index("col")
    own, mine = spans(c), spans(r)
    half = WIDTH // 2
    loads = []
    for k in range(NPAN):
        loads.append([pltpu.make_async_copy(ac.at[k], acv.at[(r + GROUPS - s) % GROUPS, k], arrive.at[4 * k + s])
                      for s, ac in ((0, ac0), (1, ac1), (2, ac2), (3, ac3))])
    copies = [pltpu.make_async_copy(*pair, arrive.at[8 + i])
              for i, pair in enumerate(((own_cols, held), (xh_in, xh), (xl_in, xl)))]
    fronts = [pltpu.make_async_copy(front.at[l], buf.at[l], arrive.at[16 + l]) for l in range(NPAN, LB)]
    for load in loads[0] + loads[1] + copies + fronts:
        load.start()
    zero = jnp.zeros((EDGE, EDGE), F32)
    for l in range(NPAN):
        for m in range(NPAN, LB):
            buf[l, :, m, :] = zero
    buf[0, :, 1, :] = zero
    buf[0, :, 0, :] = low0[mine, own]
    buf[1, :, 0, :] = across[mine, own]
    buf[1, :, 1, :] = low1[mine, own]
    store = pltpu.make_async_copy(buf.at[:NPAN], out.at[:NPAN], leave.at[0])
    store.start()
    bh[...], bl[...] = split2(across[...])
    col_end = collect(ids, 0, [(l * TILE + g, pattern[0, GROUPS + g, (l + NPAN) * GROUPS + c] > 0) for l, g in SIDE])
    all_end = collect(ids, col_end, [
        ((k * TILE + l) * TILE + m, pattern[k, (l + NPAN) * GROUPS + r, (m + NPAN) * GROUPS + c] > 0)
        for k in range(NPAN) for l in range(REST) for m in range(REST)])

    def col_product(number):
        l, g = unpair(number)
        return dot3((bh[spans(g), :], bl[spans(g), :]), (yh[0, :, spans(l)], yl[0, :, spans(l)]), NN)

    def col_target(number, change):
        l, g = unpair(number)
        acv[g, 1, :, spans(l)] = acv[g, 1, :, spans(l)] - change

    def place(number):
        row, m = unpair(number)
        return unpair(row) + (m,)

    def product(number):
        k, l, m = place(number)
        return dot3((xh[k, spans(l), :], xl[k, spans(l), :]), (yh[k, :, spans(m)], yl[k, :, spans(m)]), NN)

    def target(number, change):
        k, l, m = place(number)
        buf[l + NPAN, :, m + NPAN, :] = buf[l + NPAN, :, m + NPAN, :] - change

    for k in range(NPAN):
        for load in loads[k]:
            load.wait()
        if k == 1:
            visit(ids, 0, col_end, col_product, col_target)
        for g in range(GROUPS):
            span = slice(g * EDGE, (g + 1) * EDGE)
            sh[span, :], sl[span, :] = split2(acv[g, k])
        wh, wl = split2((inv0, inv1)[k][...])
        lc[:half, :] = dot3((wh[:half, :half], wl[:half, :half]), (sh[:half, :], sl[:half, :]), NN)
        lc[half:, :] = dot3((wh[half:, :], wl[half:, :]), (sh[...], sl[...]), NN)
        yh[k], yl[k] = split2(lc[...])
    for load in copies + fronts:
        load.wait()
    for k in range(NPAN):
        for l in range(REST):
            buf[l + NPAN, :, k, :] = held[k, l * EDGE:(l + 1) * EDGE, :]
    visit(ids, col_end, all_end, product, target)
    last = pltpu.make_async_copy(buf.at[NPAN:], out.at[NPAN:], leave.at[1])
    last.start()
    store.wait()
    last.wait()


def run(copies):
    for copy in copies:
        copy.start()
    for copy in copies:
        copy.wait()


def extract_kernel(front, ar, ac, rows, cols, sem):
    copy = pltpu.make_async_copy
    loads = [copy(front.at[NPAN:, :, k, :], rows.at[k], sem.at[k]) for k in range(NPAN)]
    for k in range(NPAN):
        for j in range(REST):
            loads.append(copy(front.at[k, :, j + NPAN, :], cols.at[k, :, j * EDGE:(j + 1) * EDGE], sem.at[len(loads)]))
    run(loads)
    run([copy(rows, ar, sem.at[0]), copy(cols, ac, sem.at[1])])


def corner_kernel(front, c0, c1, first, second, third, send0, send1, sem):
    r, c = lax.axis_index("row"), lax.axis_index("col")
    copy = pltpu.make_async_copy
    every = GROUPS * GROUPS
    loads = [copy(front.at[l, :, m, :], to, sem.at[i])
             for i, (l, m, to) in enumerate(((0, 0, first), (1, 0, send1.at[:EDGE]), (1, 1, third)))]
    for one in loads:
        one.start()
    loads[0].wait()
    pack(first[...], send0, r, c)
    stores = [copy(send0, c0.at[g], sem.at[3 + g]) for g in range(every)]
    for one in stores:
        one.start()
    loads[1].wait()
    loads[2].wait()
    pack(third[...], second, r, c)
    send1[EDGE:, :] = second[...]
    last = [copy(send1, c1.at[g], sem.at[3 + every + g]) for g in range(every)]
    for one in last:
        one.start()
    for one in stores + last:
        one.wait()


def shape(*dims):
    return jax.ShapeDtypeStruct(dims, F32)


def vmem(*dims, dtype=F32):
    return pltpu.VMEM(dims, dtype)


def call(kernel, outs, scratch=(), limit=60, **kw):
    return pl.pallas_call(
        kernel, out_shape=outs, scratch_shapes=list(scratch),
        compiler_params=pltpu.CompilerParams(vmem_limit_bytes=limit * 1024 * 1024), **kw)


def per_device(front, pattern):
    blocks = front[0, :, :, 0]
    square = shape(WIDTH, WIDTH)
    every = GROUPS * GROUPS
    away, dma = pl.BlockSpec(memory_space=pltpu.HBM), pltpu.SemaphoreType.DMA
    work = [vmem(WIDTH, WIDTH)] * 3 + [vmem(GROUPS, EDGE, EDGE)] * 2 + [dma((LB,))]
    c0, c1 = call(
        corner_kernel, [shape(every, HELD, EDGE), shape(every, EDGE + HELD, EDGE)],
        [vmem(EDGE, EDGE), vmem(HELD, EDGE), vmem(EDGE, EDGE), vmem(HELD, EDGE), vmem(EDGE + HELD, EDGE), dma((3 + 2 * every,))],
        in_specs=[away], out_specs=[away, away],
    )(blocks)
    later, c0 = lax.optimization_barrier((blocks, c0))
    got0 = lax.all_to_all(c0, ("row", "col"), 0, 0, tiled=True)
    ar, ac = call(
        extract_kernel, [shape(NPAN, REST, EDGE, EDGE), shape(NPAN, EDGE, ROWS)],
        [vmem(NPAN, REST, EDGE, EDGE), vmem(NPAN, EDGE, ROWS), dma((NPAN + NPAN * REST,))],
        in_specs=[away], out_specs=[away, away],
    )(later)
    ar = lax.all_gather(ar, "col", axis=0)
    c1, ac, got0 = lax.optimization_barrier((c1, ac, got0))
    got1 = lax.all_to_all(c1, ("row", "col"), 0, 0, tiled=True)
    low0, inv0 = call(first_kernel, [square] * 2, work, out_specs=[away] * 2)(got0)
    later, inv0 = lax.optimization_barrier((ac, inv0))
    acs = [ac] + [lax.ppermute(piece, "row", [(i, (i + s) % GROUPS) for i in range(GROUPS)])
                  for s, piece in ((1, later), (3, later), (2, ac))]
    across, low1, inv1 = call(
        second_kernel, [square] * 3,
        work + [vmem(every, EDGE, EDGE), vmem(every, HELD, EDGE), vmem(WIDTH, WIDTH), vmem(WIDTH, WIDTH), dma((4,))],
        in_specs=[away] * 2, out_specs=[away] * 3,
    )(got1, inv0)
    whole, scalars = pl.BlockSpec(memory_space=pltpu.VMEM), pl.BlockSpec(memory_space=pltpu.SMEM)
    tall, flat, bound = [(NPAN, ROWS, WIDTH)] * 2, [(NPAN, WIDTH, ROWS)] * 2, [vmem(WIDTH, WIDTH, dtype=BF16)] * 2
    xh, xl, own_cols = call(
        row_kernel, [jax.ShapeDtypeStruct(dims, BF16) for dims in tall] + [shape(NPAN, ROWS, EDGE)],
        [vmem(GROUPS, NPAN, REST, EDGE, EDGE)] + [vmem(*dims, dtype=BF16) for dims in tall]
        + [vmem(ROWS, WIDTH, dtype=BF16)] * 2 + bound
        + [vmem(ROWS, WIDTH), vmem(NPAN, ROWS, EDGE), pltpu.SMEM((32,), jnp.int32), dma((NPAN,)), dma((3 * NPAN,))],
        in_specs=[away, scalars] + [whole] * 3, out_specs=[away] * 3,
    )(ar, pattern, inv0, across, inv1)
    result = call(
        last_kernel, shape(LB, EDGE, LB, EDGE),
        [vmem(LB, EDGE, LB, EDGE), vmem(GROUPS, NPAN, EDGE, ROWS)] + [vmem(*dims, dtype=BF16) for dims in tall + flat]
        + [vmem(WIDTH, ROWS, dtype=BF16)] * 2 + bound
        + [vmem(NPAN, ROWS, EDGE), vmem(WIDTH, ROWS), pltpu.SMEM((128,), jnp.int32), dma((24,)), dma((2,))],
        in_specs=[away, scalars] + [away] * 7 + [whole] * 5, out_specs=away,
    )(blocks, pattern, xh, xl, own_cols, *acs, low0, inv0, across, low1, inv1)
    return result[None, :, :, None]


def solution(mesh):
    placed = (P("row", "front", None, "col", None, None), P("front", None, None))
    return jax.shard_map(
        per_device, mesh=mesh, in_specs=placed,
        out_specs=P("row", "front", None, "col", None, None), check_vma=False,
    )
```

```python
import functools

import jax
import jax.numpy as jnp
from jax import lax
from jax.experimental import pallas as pl
from jax.experimental.pallas import tpu as pltpu
from jax.sharding import PartitionSpec as P

F32 = jnp.float32
BF16 = jnp.bfloat16
HI = lax.Precision.HIGHEST
EDGE = 128
TILE = 8
HALF = EDGE // 2
HELD = HALF + TILE
GROUPS = 4
WIDTH = EDGE * GROUPS
LB = 8
BATCH = 4
NPAN = 2
REST = LB - NPAN
ROWS = REST * EDGE

NN = (((1,), (0,)), ((), ()))
NT = (((1,), (1,)), ((), ()))
TN = (((0,), (0,)), ((), ()))


def exact_dot(a, b, dims):
    return lax.dot_general(a, b, dims, precision=HI, preferred_element_type=F32)


def split2(x):
    high = x.astype(BF16)
    return high, (x - high.astype(F32)).astype(BF16)


def split3(x):
    high = x.astype(BF16)
    rest = x - high.astype(F32)
    mid = rest.astype(BF16)
    return high, mid, (rest - mid.astype(F32)).astype(BF16)


def dot3(a, b, dims):
    one = functools.partial(lax.dot_general, dimension_numbers=dims, preferred_element_type=F32)
    return one(a[0], b[0]) + (one(a[0], b[1]) + one(a[1], b[0]))


def spread(x):
    return jnp.broadcast_to(x, (TILE, EDGE))


def factor_block(a, w):
    sub = lax.broadcasted_iota(jnp.int32, (TILE, EDGE), 0)
    count = EDGE // TILE

    def tile(p):
        return slice(TILE * p, TILE * (p + 1))

    def columns(x, p):
        return [spread(x[:, TILE * p + q:TILE * p + q + 1]) for q in range(TILE)]

    rows = [(a[tile(p), :], w[tile(p), :]) for p in range(2)]
    cols = columns(rows[0][0], 0)
    for p in range(count):
        if p + 2 < count:
            rows.append((a[tile(p + 2), :], w[tile(p + 2), :]))
        below = [columns(left, p) for left, _ in rows[1:]]
        corner = columns(rows[1][0], p + 1) if len(rows) > 1 else None
        invs = jnp.zeros((TILE, EDGE), F32)
        pivot = spread(cols[0][:1, :])
        for q in range(TILE):
            inv = 1.0 / pivot
            if q + 1 < TILE:
                beside = spread(cols[q + 1][q:q + 1, :])
                pivot = spread(cols[q + 1][q + 1:q + 2, :]) - (beside * beside) * inv
            invs = jnp.where(sub == q, inv, invs)
            factors = [jnp.where(sub > q, cols[q], 0.0) * inv] + [one[q] * inv for one in below]
            left, right = (spread(x[q:q + 1, :]) for x in rows[0])
            rows = [(x - m * left, y - m * right) for (x, y), m in zip(rows, factors)]
            if corner is not None:
                corner = [x - factors[1] * spread(below[0][q][t:t + 1, :]) for t, x in enumerate(corner)]
            for t in range(q + 1, TILE):
                across = spread(cols[t][q:q + 1, :])
                for one, m in zip([cols] + below, factors):
                    one[t] = one[t] - m * across
        root = lax.rsqrt(invs) * invs
        left, right = rows[0][0] * root, rows[0][1] * root
        a[tile(p), :], w[tile(p), :] = left, right
        low = TILE * (p + 3)
        if low < EDGE:
            h, m, l = split3(left)
            vh, vm, vl = split3(right)
            uh, um, ul = (jnp.concatenate(pair, 1) for pair in ((h, vh), (m, vm), (l, vl)))
            lhs = jnp.concatenate([h, h, m, h, m, l], 0)
            rhs = jnp.concatenate([uh, um, uh, ul, um, uh], 0)
            change = lax.dot_general(lhs, rhs, TN, preferred_element_type=F32)
            a[low:, :] = a[low:, :] - change[low:, :EDGE]
            w[low:, :] = w[low:, :] - change[low:, EDGE:]
        rows, cols = rows[1:], corner


def factor_panel(s, lower, inverse, a, w, low_out, inv_out, sem):
    ri = lax.broadcasted_iota(jnp.int32, (EDGE, EDGE), 0)
    ci = lax.broadcasted_iota(jnp.int32, (EDGE, EDGE), 1)
    copies = []
    for k in range(GROUPS):
        here = slice(k * EDGE, (k + 1) * EDGE)
        below = slice((k + 1) * EDGE, WIDTH)
        before = slice(0, k * EDGE)
        if k + 1 < GROUPS:
            lower[here, below] = jnp.zeros((EDGE, WIDTH - (k + 1) * EDGE), F32)
            inverse[here, below] = jnp.zeros((EDGE, WIDTH - (k + 1) * EDGE), F32)
        a[k] = s[here, here]
        w[k] = jnp.where(ri == ci, 1.0, 0.0)
        factor_block(a.at[k], w.at[k])
        d = w[k]
        if k + 1 < GROUPS:
            part = exact_dot(s[below, here], d, NT)
            lower[below, here] = part
            s[below, below] = s[below, below] - exact_dot(part, part, NT)
        lower[here, here] = jnp.where(ri <= ci, a[k], 0.0).T
        inverse[here, here] = d
        if k > 0:
            part = exact_dot(lower[here, before], inverse[before, before], NN)
            inverse[here, before] = -exact_dot(d, part, NN)
        for i, (held, to) in enumerate(((lower, low_out), (inverse, inv_out))):
            copies.append(pltpu.make_async_copy(held.at[here], to.at[here], sem.at[2 * k + i]))
            copies[-1].start()
    for copy in copies:
        copy.wait()


def pack(block, ref, r, c):
    row = lax.broadcasted_iota(jnp.int32, (HALF, EDGE), 0)
    lane = lax.broadcasted_iota(jnp.int32, (HALF, EDGE), 1)
    top, low = block[:HALF], block[HALF:]
    diagonal = jnp.where(lane - HALF > row, pltpu.roll(top, HALF, 1), low)
    ref[:HALF, :] = jnp.where(r == c, diagonal, jnp.where(r > c, top, block.T[HALF:]))
    ref[HALF:HELD, :] = spread(jnp.sum(jnp.where(lane == row, top, 0.0), axis=0, keepdims=True))


def unpack_diagonal(got):
    row = lax.broadcasted_iota(jnp.int32, (EDGE, EDGE), 0)
    lane = lax.broadcasted_iota(jnp.int32, (EDGE, EDGE), 1)
    body = got[:HALF]
    some = jnp.concatenate([pltpu.roll(body, HALF, 1), body], 0)
    kept = ((row >= HALF) & (lane <= row)) | ((lane < HALF) & (row < lane))
    whole = jnp.where(kept, some, some.T)
    return jnp.where((row == lane) & (row < HALF), jnp.broadcast_to(got[HALF:HALF + 1], (EDGE, EDGE)), whole)


def unpack(got, s):
    for r in range(GROUPS):
        for c in range(r):
            span = slice(c * EDGE, (c + 1) * EDGE)
            s[r * EDGE:r * EDGE + HALF, span] = got[r * GROUPS + c, 0:HALF]
            s[r * EDGE + HALF:(r + 1) * EDGE, span] = got[c * GROUPS + r, 0:HALF]
        span = slice(r * EDGE, (r + 1) * EDGE)
        s[span, span] = unpack_diagonal(got[r * GROUPS + r, 0:HELD])


def first_kernel(got, low_out, inv_out, s, lower, inverse, a, w, sem):
    unpack(got, s)
    factor_panel(s, lower, inverse, a, w, low_out, inv_out, sem)


def second_kernel(got, inverse0, across_out, low_out, inv_out, s, lower, inverse, a, w, sem, rect, square, across, invs, sem2):
    loads = [pltpu.make_async_copy(*pair, sem2.at[i]) for i, pair in enumerate(
        ((inverse0, invs), (got.at[:, :EDGE], rect), (got.at[:, EDGE:], square)))]
    for load in loads:
        load.start()
    loads[0].wait()
    inv = split2(invs[...])
    loads[1].wait()
    for r in range(GROUPS):
        for c in range(GROUPS):
            s[r * EDGE:(r + 1) * EDGE, c * EDGE:(c + 1) * EDGE] = rect[r * GROUPS + c]
    across[...] = dot3(split2(s[...]), inv, NT)
    store = pltpu.make_async_copy(across, across_out, sem2.at[3])
    store.start()
    loads[2].wait()
    unpack(square, s)
    part = split2(across[...])
    s[...] = s[...] - dot3(part, part, NT)
    factor_panel(s, lower, inverse, a, w, low_out, inv_out, sem)
    store.wait()


def collect(ids, at, flags):
    for number, flag in flags:
        ids[at] = number
        at = at + jnp.where(flag, 1, 0)
    return at


def visit(ids, first, last, product, target):
    def step(i, _):
        slots = [first + i * BATCH + j for j in range(BATCH)]
        numbers = [ids[jnp.minimum(slot, last - 1)] for slot in slots]
        changes = [jnp.where(slot < last, product(number), 0.0) for slot, number in zip(slots, numbers)]
        for number, change in zip(numbers, changes):
            target(number, change)
        return 0

    lax.fori_loop(0, lax.div(last - first + BATCH - 1, BATCH), step, 0)


def spans(i):
    return pl.ds(pl.multiple_of(i * EDGE, EDGE), EDGE)


def unpair(number):
    return lax.div(number, TILE), lax.rem(number, TILE)


SIDE = [(l, g) for l in range(REST) for g in range(GROUPS)]


def row_kernel(ar, pattern, inv0, across, inv1, xh_out, xl_out, mine_out,
               arv, xh, xl, th, tl, bh, bl, lr, mine, ids, arrive, leave):
    r, own = lax.axis_index("row"), spans(lax.axis_index("col"))
    half = WIDTH // 2
    loads = [pltpu.make_async_copy(ar.at[:, k], arv.at[:, k], arrive.at[k]) for k in range(NPAN)]
    for load in loads:
        load.start()
    bh[...], bl[...] = split2(across[...])
    end = collect(ids, 0, [(l * TILE + g, pattern[0, (l + NPAN) * GROUPS + r, GROUPS + g] > 0) for l, g in SIDE])

    def product(number):
        l, g = unpair(number)
        return dot3((xh[0, spans(l), :], xl[0, spans(l), :]), (bh[spans(g), :], bl[spans(g), :]), NT)

    def target(number, change):
        l, g = unpair(number)
        arv[g, 1, l] = arv[g, 1, l] - change

    stores = []
    for k in range(NPAN):
        loads[k].wait()
        if k == 1:
            visit(ids, 0, end, product, target)
        for g in range(GROUPS):
            span = slice(g * EDGE, (g + 1) * EDGE)
            th[:, span], tl[:, span] = split2(arv[g, k].reshape(ROWS, EDGE))
        wh, wl = split2((inv0, inv1)[k][...])
        lr[:, :half] = dot3((th[:, :half], tl[:, :half]), (wh[:half, :half], wl[:half, :half]), NT)
        lr[:, half:] = dot3((th[...], tl[...]), (wh[half:, :], wl[half:, :]), NT)
        xh[k], xl[k] = split2(lr[...])
        mine[k] = lr[:, own]
        for i, (held, to) in enumerate(((xh, xh_out), (xl, xl_out), (mine, mine_out))):
            stores.append(pltpu.make_async_copy(held.at[k], to.at[k], leave.at[3 * k + i]))
            stores[-1].start()
    for store in stores:
        store.wait()


def last_kernel(front, pattern, xh_in, xl_in, own_cols, ac0, ac1, ac3, ac2, low0, inv0, across, low1, inv1, out,
                buf, acv, xh, xl, yh, yl, sh, sl, bh, bl, held, lc, ids, arrive, leave):
    r, c = lax.axis_index("row"), lax.axis_index("col")
    own, mine = spans(c), spans(r)
    half = WIDTH // 2
    loads = []
    for k in range(NPAN):
        loads.append([pltpu.make_async_copy(ac.at[k], acv.at[(r + GROUPS - s) % GROUPS, k], arrive.at[4 * k + s])
                      for s, ac in ((0, ac0), (1, ac1), (2, ac2), (3, ac3))])
    copies = [pltpu.make_async_copy(*pair, arrive.at[8 + i])
              for i, pair in enumerate(((own_cols, held), (xh_in, xh), (xl_in, xl)))]
    fronts = [pltpu.make_async_copy(front.at[l], buf.at[l], arrive.at[16 + l]) for l in range(NPAN, LB)]
    for load in loads[0] + loads[1]:
        load.start()
    zero = jnp.zeros((EDGE, EDGE), F32)
    for l in range(NPAN):
        for m in range(NPAN, LB):
            buf[l, :, m, :] = zero
    buf[0, :, 1, :] = zero
    buf[0, :, 0, :] = low0[mine, own]
    buf[1, :, 0, :] = across[mine, own]
    buf[1, :, 1, :] = low1[mine, own]
    store = pltpu.make_async_copy(buf.at[:NPAN], out.at[:NPAN], leave.at[0])
    store.start()
    bh[...], bl[...] = split2(across[...])
    col_end = collect(ids, 0, [(l * TILE + g, pattern[0, GROUPS + g, (l + NPAN) * GROUPS + c] > 0) for l, g in SIDE])
    all_end = collect(ids, col_end, [
        ((k * TILE + l) * TILE + m, pattern[k, (l + NPAN) * GROUPS + r, (m + NPAN) * GROUPS + c] > 0)
        for k in range(NPAN) for l in range(REST) for m in range(REST)])

    def col_product(number):
        l, g = unpair(number)
        return dot3((bh[spans(g), :], bl[spans(g), :]), (yh[0, :, spans(l)], yl[0, :, spans(l)]), NN)

    def col_target(number, change):
        l, g = unpair(number)
        acv[g, 1, :, spans(l)] = acv[g, 1, :, spans(l)] - change

    def place(number):
        row, m = unpair(number)
        return unpair(row) + (m,)

    def product(number):
        k, l, m = place(number)
        return dot3((xh[k, spans(l), :], xl[k, spans(l), :]), (yh[k, :, spans(m)], yl[k, :, spans(m)]), NN)

    def target(number, change):
        k, l, m = place(number)
        buf[l + NPAN, :, m + NPAN, :] = buf[l + NPAN, :, m + NPAN, :] - change

    for k in range(NPAN):
        for load in loads[k]:
            load.wait()
        if k == 0:
            for load in copies + fronts:
                load.start()
        if k == 1:
            visit(ids, 0, col_end, col_product, col_target)
        for g in range(GROUPS):
            span = slice(g * EDGE, (g + 1) * EDGE)
            sh[span, :], sl[span, :] = split2(acv[g, k])
        wh, wl = split2((inv0, inv1)[k][...])
        lc[:half, :] = dot3((wh[:half, :half], wl[:half, :half]), (sh[:half, :], sl[:half, :]), NN)
        lc[half:, :] = dot3((wh[half:, :], wl[half:, :]), (sh[...], sl[...]), NN)
        yh[k], yl[k] = split2(lc[...])
    for load in copies + fronts:
        load.wait()
    for k in range(NPAN):
        for l in range(REST):
            buf[l + NPAN, :, k, :] = held[k, l * EDGE:(l + 1) * EDGE, :]
    visit(ids, col_end, all_end, product, target)
    last = pltpu.make_async_copy(buf.at[NPAN:], out.at[NPAN:], leave.at[1])
    last.start()
    store.wait()
    last.wait()


def run(copies):
    for copy in copies:
        copy.start()
    for copy in copies:
        copy.wait()


def extract_kernel(front, ar, ac, rows, cols, sem):
    copy = pltpu.make_async_copy
    loads = [copy(front.at[NPAN:, :, k, :], rows.at[k], sem.at[k]) for k in range(NPAN)]
    for k in range(NPAN):
        for j in range(REST):
            loads.append(copy(front.at[k, :, j + NPAN, :], cols.at[k, :, j * EDGE:(j + 1) * EDGE], sem.at[len(loads)]))
    run(loads)
    run([copy(rows, ar, sem.at[0]), copy(cols, ac, sem.at[1])])


def corner_kernel(front, c0, c1, first, second, third, send0, send1, sem):
    r, c = lax.axis_index("row"), lax.axis_index("col")
    copy = pltpu.make_async_copy
    every = GROUPS * GROUPS
    loads = [copy(front.at[l, :, m, :], to, sem.at[i])
             for i, (l, m, to) in enumerate(((0, 0, first), (1, 0, send1.at[:EDGE]), (1, 1, third)))]
    for one in loads:
        one.start()
    loads[0].wait()
    pack(first[...], send0, r, c)
    stores = [copy(send0, c0.at[g], sem.at[3 + g]) for g in range(every)]
    for one in stores:
        one.start()
    loads[1].wait()
    loads[2].wait()
    pack(third[...], second, r, c)
    send1[EDGE:, :] = second[...]
    last = [copy(send1, c1.at[g], sem.at[3 + every + g]) for g in range(every)]
    for one in last:
        one.start()
    for one in stores + last:
        one.wait()


def shape(*dims):
    return jax.ShapeDtypeStruct(dims, F32)


def vmem(*dims, dtype=F32):
    return pltpu.VMEM(dims, dtype)


def call(kernel, outs, scratch=(), limit=60, **kw):
    return pl.pallas_call(
        kernel, out_shape=outs, scratch_shapes=list(scratch),
        compiler_params=pltpu.CompilerParams(vmem_limit_bytes=limit * 1024 * 1024), **kw)


def per_device(front, pattern):
    blocks = front[0, :, :, 0]
    square = shape(WIDTH, WIDTH)
    every = GROUPS * GROUPS
    away, dma = pl.BlockSpec(memory_space=pltpu.HBM), pltpu.SemaphoreType.DMA
    work = [vmem(WIDTH, WIDTH)] * 3 + [vmem(GROUPS, EDGE, EDGE)] * 2 + [dma((LB,))]
    c0, c1 = call(
        corner_kernel, [shape(every, HELD, EDGE), shape(every, EDGE + HELD, EDGE)],
        [vmem(EDGE, EDGE), vmem(HELD, EDGE), vmem(EDGE, EDGE), vmem(HELD, EDGE), vmem(EDGE + HELD, EDGE), dma((3 + 2 * every,))],
        in_specs=[away], out_specs=[away, away],
    )(blocks)
    later, c0 = lax.optimization_barrier((blocks, c0))
    got0 = lax.all_to_all(c0, ("row", "col"), 0, 0, tiled=True)
    ar, ac = call(
        extract_kernel, [shape(NPAN, REST, EDGE, EDGE), shape(NPAN, EDGE, ROWS)],
        [vmem(NPAN, REST, EDGE, EDGE), vmem(NPAN, EDGE, ROWS), dma((NPAN + NPAN * REST,))],
        in_specs=[away], out_specs=[away, away],
    )(later)
    ar = lax.all_gather(ar, "col", axis=0)
    c1, got0 = lax.optimization_barrier((c1, got0))
    got1 = lax.all_to_all(c1, ("row", "col"), 0, 0, tiled=True)
    low0, inv0 = call(first_kernel, [square] * 2, work, out_specs=[away] * 2)(got0)
    ac, got1, inv0 = lax.optimization_barrier((ac, got1, inv0))
    acs = [ac] + [lax.ppermute(ac, "row", [(i, (i + s) % GROUPS) for i in range(GROUPS)]) for s in (1, 3, 2)]
    across, low1, inv1 = call(
        second_kernel, [square] * 3,
        work + [vmem(every, EDGE, EDGE), vmem(every, HELD, EDGE), vmem(WIDTH, WIDTH), vmem(WIDTH, WIDTH), dma((4,))],
        in_specs=[away] * 2, out_specs=[away] * 3,
    )(got1, inv0)
    whole, scalars = pl.BlockSpec(memory_space=pltpu.VMEM), pl.BlockSpec(memory_space=pltpu.SMEM)
    tall, flat, bound = [(NPAN, ROWS, WIDTH)] * 2, [(NPAN, WIDTH, ROWS)] * 2, [vmem(WIDTH, WIDTH, dtype=BF16)] * 2
    xh, xl, own_cols = call(
        row_kernel, [jax.ShapeDtypeStruct(dims, BF16) for dims in tall] + [shape(NPAN, ROWS, EDGE)],
        [vmem(GROUPS, NPAN, REST, EDGE, EDGE)] + [vmem(*dims, dtype=BF16) for dims in tall]
        + [vmem(ROWS, WIDTH, dtype=BF16)] * 2 + bound
        + [vmem(ROWS, WIDTH), vmem(NPAN, ROWS, EDGE), pltpu.SMEM((32,), jnp.int32), dma((NPAN,)), dma((3 * NPAN,))],
        in_specs=[away, scalars] + [whole] * 3, out_specs=[away] * 3,
    )(ar, pattern, inv0, across, inv1)
    result = call(
        last_kernel, shape(LB, EDGE, LB, EDGE),
        [vmem(LB, EDGE, LB, EDGE), vmem(GROUPS, NPAN, EDGE, ROWS)] + [vmem(*dims, dtype=BF16) for dims in tall + flat]
        + [vmem(WIDTH, ROWS, dtype=BF16)] * 2 + bound
        + [vmem(NPAN, ROWS, EDGE), vmem(WIDTH, ROWS), pltpu.SMEM((128,), jnp.int32), dma((24,)), dma((2,))],
        in_specs=[away, scalars] + [away] * 7 + [whole] * 5, out_specs=away,
    )(blocks, pattern, xh, xl, own_cols, *acs, low0, inv0, across, low1, inv1)
    return result[None, :, :, None]


def solution(mesh):
    placed = (P("row", "front", None, "col", None, None), P("front", None, None))
    return jax.shard_map(
        per_device, mesh=mesh, in_specs=placed,
        out_specs=P("row", "front", None, "col", None, None), check_vma=False,
    )
```

```python
import functools

import jax
import jax.numpy as jnp
from jax import lax
from jax.experimental import pallas as pl
from jax.experimental.pallas import tpu as pltpu
from jax.sharding import PartitionSpec as P

F32 = jnp.float32
BF16 = jnp.bfloat16
HI = lax.Precision.HIGHEST
EDGE = 128
TILE = 8
HALF = EDGE // 2
HELD = HALF + TILE
GROUPS = 4
WIDTH = EDGE * GROUPS
LB = 8
BATCH = 4
NPAN = 2
REST = LB - NPAN
ROWS = REST * EDGE

NN = (((1,), (0,)), ((), ()))
NT = (((1,), (1,)), ((), ()))
TN = (((0,), (0,)), ((), ()))


def exact_dot(a, b, dims):
    return lax.dot_general(a, b, dims, precision=HI, preferred_element_type=F32)


def split2(x):
    high = x.astype(BF16)
    return high, (x - high.astype(F32)).astype(BF16)


def split3(x):
    high = x.astype(BF16)
    rest = x - high.astype(F32)
    mid = rest.astype(BF16)
    return high, mid, (rest - mid.astype(F32)).astype(BF16)


def dot3(a, b, dims):
    one = functools.partial(lax.dot_general, dimension_numbers=dims, preferred_element_type=F32)
    return one(a[0], b[0]) + (one(a[0], b[1]) + one(a[1], b[0]))


def spread(x):
    return jnp.broadcast_to(x, (TILE, EDGE))


def factor_block(a, w):
    sub = lax.broadcasted_iota(jnp.int32, (TILE, EDGE), 0)
    count = EDGE // TILE

    def tile(p):
        return slice(TILE * p, TILE * (p + 1))

    def columns(x, p):
        return [spread(x[:, TILE * p + q:TILE * p + q + 1]) for q in range(TILE)]

    rows = [(a[tile(p), :], w[tile(p), :]) for p in range(2)]
    cols = columns(rows[0][0], 0)
    for p in range(count):
        if p + 2 < count:
            rows.append((a[tile(p + 2), :], w[tile(p + 2), :]))
        below = [columns(left, p) for left, _ in rows[1:]]
        corner = columns(rows[1][0], p + 1) if len(rows) > 1 else None
        invs = jnp.zeros((TILE, EDGE), F32)
        pivot = spread(cols[0][:1, :])
        for q in range(TILE):
            inv = 1.0 / pivot
            if q + 1 < TILE:
                beside = spread(cols[q + 1][q:q + 1, :])
                pivot = spread(cols[q + 1][q + 1:q + 2, :]) - (beside * beside) * inv
            invs = jnp.where(sub == q, inv, invs)
            factors = [jnp.where(sub > q, cols[q], 0.0) * inv] + [one[q] * inv for one in below]
            left, right = (spread(x[q:q + 1, :]) for x in rows[0])
            rows = [(x - m * left, y - m * right) for (x, y), m in zip(rows, factors)]
            if corner is not None:
                corner = [x - factors[1] * spread(below[0][q][t:t + 1, :]) for t, x in enumerate(corner)]
            for t in range(q + 1, TILE):
                across = spread(cols[t][q:q + 1, :])
                for one, m in zip([cols] + below, factors):
                    one[t] = one[t] - m * across
        root = lax.rsqrt(invs) * invs
        left, right = rows[0][0] * root, rows[0][1] * root
        a[tile(p), :], w[tile(p), :] = left, right
        low = TILE * (p + 3)
        if low < EDGE:
            h, m, l = split3(left)
            vh, vm, vl = split3(right)
            uh, um, ul = (jnp.concatenate(pair, 1) for pair in ((h, vh), (m, vm), (l, vl)))
            lhs = jnp.concatenate([h, h, m, h, m, l], 0)
            rhs = jnp.concatenate([uh, um, uh, ul, um, uh], 0)
            change = lax.dot_general(lhs, rhs, TN, preferred_element_type=F32)
            a[low:, :] = a[low:, :] - change[low:, :EDGE]
            w[low:, :] = w[low:, :] - change[low:, EDGE:]
        rows, cols = rows[1:], corner


def factor_panel(s, lower, inverse, a, w, low_out, inv_out, sem):
    ri = lax.broadcasted_iota(jnp.int32, (EDGE, EDGE), 0)
    ci = lax.broadcasted_iota(jnp.int32, (EDGE, EDGE), 1)
    copies = []
    for k in range(GROUPS):
        here = slice(k * EDGE, (k + 1) * EDGE)
        below = slice((k + 1) * EDGE, WIDTH)
        before = slice(0, k * EDGE)
        if k + 1 < GROUPS:
            lower[here, below] = jnp.zeros((EDGE, WIDTH - (k + 1) * EDGE), F32)
            inverse[here, below] = jnp.zeros((EDGE, WIDTH - (k + 1) * EDGE), F32)
        a[k] = s[here, here]
        w[k] = jnp.where(ri == ci, 1.0, 0.0)
        factor_block(a.at[k], w.at[k])
        d = w[k]
        if k + 1 < GROUPS:
            part = exact_dot(s[below, here], d, NT)
            lower[below, here] = part
            s[below, below] = s[below, below] - exact_dot(part, part, NT)
        lower[here, here] = jnp.where(ri <= ci, a[k], 0.0).T
        inverse[here, here] = d
        if k > 0:
            part = exact_dot(lower[here, before], inverse[before, before], NN)
            inverse[here, before] = -exact_dot(d, part, NN)
        for i, (held, to) in enumerate(((lower, low_out), (inverse, inv_out))):
            copies.append(pltpu.make_async_copy(held.at[here], to.at[here], sem.at[2 * k + i]))
            copies[-1].start()
    for copy in copies:
        copy.wait()


def pack(block, ref, r, c):
    row = lax.broadcasted_iota(jnp.int32, (HALF, EDGE), 0)
    lane = lax.broadcasted_iota(jnp.int32, (HALF, EDGE), 1)
    top, low = block[:HALF], block[HALF:]
    diagonal = jnp.where(lane - HALF > row, pltpu.roll(top, HALF, 1), low)
    ref[:HALF, :] = jnp.where(r == c, diagonal, jnp.where(r > c, top, block.T[HALF:]))
    ref[HALF:HELD, :] = spread(jnp.sum(jnp.where(lane == row, top, 0.0), axis=0, keepdims=True))


def unpack_diagonal(got):
    row = lax.broadcasted_iota(jnp.int32, (EDGE, EDGE), 0)
    lane = lax.broadcasted_iota(jnp.int32, (EDGE, EDGE), 1)
    body = got[:HALF]
    some = jnp.concatenate([pltpu.roll(body, HALF, 1), body], 0)
    kept = ((row >= HALF) & (lane <= row)) | ((lane < HALF) & (row < lane))
    whole = jnp.where(kept, some, some.T)
    return jnp.where((row == lane) & (row < HALF), jnp.broadcast_to(got[HALF:HALF + 1], (EDGE, EDGE)), whole)


def unpack(got, s):
    for r in range(GROUPS):
        for c in range(r):
            span = slice(c * EDGE, (c + 1) * EDGE)
            s[r * EDGE:r * EDGE + HALF, span] = got[r * GROUPS + c, 0:HALF]
            s[r * EDGE + HALF:(r + 1) * EDGE, span] = got[c * GROUPS + r, 0:HALF]
        span = slice(r * EDGE, (r + 1) * EDGE)
        s[span, span] = unpack_diagonal(got[r * GROUPS + r, 0:HELD])


def first_kernel(got, low_out, inv_out, s, lower, inverse, a, w, sem):
    unpack(got, s)
    factor_panel(s, lower, inverse, a, w, low_out, inv_out, sem)


def second_kernel(got, inverse0, across_out, low_out, inv_out, s, lower, inverse, a, w, sem, rect, square, across, invs, sem2):
    loads = [pltpu.make_async_copy(*pair, sem2.at[i]) for i, pair in enumerate(
        ((inverse0, invs), (got.at[:, :EDGE], rect), (got.at[:, EDGE:], square)))]
    for load in loads:
        load.start()
    loads[0].wait()
    inv = split2(invs[...])
    loads[1].wait()
    for r in range(GROUPS):
        for c in range(GROUPS):
            s[r * EDGE:(r + 1) * EDGE, c * EDGE:(c + 1) * EDGE] = rect[r * GROUPS + c]
    across[...] = dot3(split2(s[...]), inv, NT)
    store = pltpu.make_async_copy(across, across_out, sem2.at[3])
    store.start()
    loads[2].wait()
    unpack(square, s)
    part = split2(across[...])
    s[...] = s[...] - dot3(part, part, NT)
    factor_panel(s, lower, inverse, a, w, low_out, inv_out, sem)
    store.wait()


def collect(ids, at, flags):
    for number, flag in flags:
        ids[at] = number
        at = at + jnp.where(flag, 1, 0)
    return at


def visit(ids, first, last, product, target):
    def step(i, _):
        slots = [first + i * BATCH + j for j in range(BATCH)]
        numbers = [ids[jnp.minimum(slot, last - 1)] for slot in slots]
        changes = [jnp.where(slot < last, product(number), 0.0) for slot, number in zip(slots, numbers)]
        for number, change in zip(numbers, changes):
            target(number, change)
        return 0

    lax.fori_loop(0, lax.div(last - first + BATCH - 1, BATCH), step, 0)


def spans(i):
    return pl.ds(pl.multiple_of(i * EDGE, EDGE), EDGE)


def unpair(number):
    return lax.div(number, TILE), lax.rem(number, TILE)


SIDE = [(l, g) for l in range(REST) for g in range(GROUPS)]


def row_kernel(ar, pattern, inv0, across, inv1, xh_out, xl_out, mine_out,
               arv, xh, xl, th, tl, bh, bl, lr, mine, ids, arrive, leave):
    r, own = lax.axis_index("row"), spans(lax.axis_index("col"))
    half = WIDTH // 2
    loads = [pltpu.make_async_copy(ar.at[:, k], arv.at[:, k], arrive.at[k]) for k in range(NPAN)]
    for load in loads:
        load.start()
    bh[...], bl[...] = split2(across[...])
    end = collect(ids, 0, [(l * TILE + g, pattern[0, (l + NPAN) * GROUPS + r, GROUPS + g] > 0) for l, g in SIDE])

    def product(number):
        l, g = unpair(number)
        return dot3((xh[0, spans(l), :], xl[0, spans(l), :]), (bh[spans(g), :], bl[spans(g), :]), NT)

    def target(number, change):
        l, g = unpair(number)
        arv[g, 1, l] = arv[g, 1, l] - change

    stores = []
    for k in range(NPAN):
        loads[k].wait()
        if k == 1:
            visit(ids, 0, end, product, target)
        for g in range(GROUPS):
            span = slice(g * EDGE, (g + 1) * EDGE)
            th[:, span], tl[:, span] = split2(arv[g, k].reshape(ROWS, EDGE))
        wh, wl = split2((inv0, inv1)[k][...])
        lr[:, :half] = dot3((th[:, :half], tl[:, :half]), (wh[:half, :half], wl[:half, :half]), NT)
        lr[:, half:] = dot3((th[...], tl[...]), (wh[half:, :], wl[half:, :]), NT)
        xh[k], xl[k] = split2(lr[...])
        mine[k] = lr[:, own]
        for i, (held, to) in enumerate(((xh, xh_out), (xl, xl_out), (mine, mine_out))):
            stores.append(pltpu.make_async_copy(held.at[k], to.at[k], leave.at[3 * k + i]))
            stores[-1].start()
    for store in stores:
        store.wait()


def last_kernel(front, pattern, xh_in, xl_in, own_cols, ac0, ac1, ac3, ac2, low0, inv0, across, low1, inv1, out,
                buf, acv, xh, xl, yh, yl, sh, sl, bh, bl, held, lc, ids, arrive, leave):
    r, c = lax.axis_index("row"), lax.axis_index("col")
    own, mine = spans(c), spans(r)
    half = WIDTH // 2
    loads = []
    for k in range(NPAN):
        loads.append([pltpu.make_async_copy(ac.at[k], acv.at[(r + GROUPS - s) % GROUPS, k], arrive.at[4 * k + s])
                      for s, ac in ((0, ac0), (1, ac1), (2, ac2), (3, ac3))])
    copies = [pltpu.make_async_copy(*pair, arrive.at[8 + i])
              for i, pair in enumerate(((own_cols, held), (xh_in, xh), (xl_in, xl)))]
    fronts = [pltpu.make_async_copy(front.at[l], buf.at[l], arrive.at[16 + l]) for l in range(NPAN, LB)]
    for load in loads[0] + loads[1] + copies + fronts:
        load.start()
    zero = jnp.zeros((EDGE, EDGE), F32)
    for l in range(NPAN):
        for m in range(NPAN, LB):
            buf[l, :, m, :] = zero
    buf[0, :, 1, :] = zero
    buf[0, :, 0, :] = low0[mine, own]
    buf[1, :, 0, :] = across[mine, own]
    buf[1, :, 1, :] = low1[mine, own]
    store = pltpu.make_async_copy(buf.at[:NPAN], out.at[:NPAN], leave.at[0])
    store.start()
    bh[...], bl[...] = split2(across[...])
    col_end = collect(ids, 0, [(l * TILE + g, pattern[0, GROUPS + g, (l + NPAN) * GROUPS + c] > 0) for l, g in SIDE])
    all_end = collect(ids, col_end, [
        ((k * TILE + l) * TILE + m, pattern[k, (l + NPAN) * GROUPS + r, (m + NPAN) * GROUPS + c] > 0)
        for k in range(NPAN) for l in range(REST) for m in range(REST)])

    def col_product(number):
        l, g = unpair(number)
        return dot3((bh[spans(g), :], bl[spans(g), :]), (yh[0, :, spans(l)], yl[0, :, spans(l)]), NN)

    def col_target(number, change):
        l, g = unpair(number)
        acv[g, 1, :, spans(l)] = acv[g, 1, :, spans(l)] - change

    def place(number):
        row, m = unpair(number)
        return unpair(row) + (m,)

    def product(number):
        k, l, m = place(number)
        return dot3((xh[k, spans(l), :], xl[k, spans(l), :]), (yh[k, :, spans(m)], yl[k, :, spans(m)]), NN)

    def target(number, change):
        k, l, m = place(number)
        buf[l + NPAN, :, m + NPAN, :] = buf[l + NPAN, :, m + NPAN, :] - change

    for k in range(NPAN):
        for load in loads[k]:
            load.wait()
        if k == 1:
            visit(ids, 0, col_end, col_product, col_target)
        for g in range(GROUPS):
            span = slice(g * EDGE, (g + 1) * EDGE)
            sh[span, :], sl[span, :] = split2(acv[g, k])
        wh, wl = split2((inv0, inv1)[k][...])
        lc[:half, :] = dot3((wh[:half, :half], wl[:half, :half]), (sh[:half, :], sl[:half, :]), NN)
        lc[half:, :] = dot3((wh[half:, :], wl[half:, :]), (sh[...], sl[...]), NN)
        yh[k], yl[k] = split2(lc[...])
    for load in copies + fronts:
        load.wait()
    for k in range(NPAN):
        for l in range(REST):
            buf[l + NPAN, :, k, :] = held[k, l * EDGE:(l + 1) * EDGE, :]
    visit(ids, col_end, all_end, product, target)
    last = pltpu.make_async_copy(buf.at[NPAN:], out.at[NPAN:], leave.at[1])
    last.start()
    store.wait()
    last.wait()


def run(copies):
    for copy in copies:
        copy.start()
    for copy in copies:
        copy.wait()


def extract_kernel(front, ar, ac, rows, cols, sem):
    copy = pltpu.make_async_copy
    loads = [copy(front.at[NPAN:, :, k, :], rows.at[k], sem.at[k]) for k in range(NPAN)]
    for k in range(NPAN):
        for j in range(REST):
            loads.append(copy(front.at[k, :, j + NPAN, :], cols.at[k, :, j * EDGE:(j + 1) * EDGE], sem.at[len(loads)]))
    run(loads)
    run([copy(rows, ar, sem.at[0]), copy(cols, ac, sem.at[1])])


def corner_kernel(front, c0, c1, first, second, third, send0, send1, sem):
    r, c = lax.axis_index("row"), lax.axis_index("col")
    copy = pltpu.make_async_copy
    every = GROUPS * GROUPS
    loads = [copy(front.at[l, :, m, :], to, sem.at[i])
             for i, (l, m, to) in enumerate(((0, 0, first), (1, 0, send1.at[:EDGE]), (1, 1, third)))]
    for one in loads:
        one.start()
    loads[0].wait()
    pack(first[...], send0, r, c)
    stores = [copy(send0, c0.at[g], sem.at[3 + g]) for g in range(every)]
    for one in stores:
        one.start()
    loads[1].wait()
    loads[2].wait()
    pack(third[...], second, r, c)
    send1[EDGE:, :] = second[...]
    last = [copy(send1, c1.at[g], sem.at[3 + every + g]) for g in range(every)]
    for one in last:
        one.start()
    for one in stores + last:
        one.wait()


def shape(*dims):
    return jax.ShapeDtypeStruct(dims, F32)


def vmem(*dims, dtype=F32):
    return pltpu.VMEM(dims, dtype)


def call(kernel, outs, scratch=(), limit=60, **kw):
    return pl.pallas_call(
        kernel, out_shape=outs, scratch_shapes=list(scratch),
        compiler_params=pltpu.CompilerParams(vmem_limit_bytes=limit * 1024 * 1024), **kw)


def per_device(front, pattern):
    blocks = front[0, :, :, 0]
    square = shape(WIDTH, WIDTH)
    every = GROUPS * GROUPS
    away, dma = pl.BlockSpec(memory_space=pltpu.HBM), pltpu.SemaphoreType.DMA
    work = [vmem(WIDTH, WIDTH)] * 3 + [vmem(GROUPS, EDGE, EDGE)] * 2 + [dma((LB,))]
    c0, c1 = call(
        corner_kernel, [shape(every, HELD, EDGE), shape(every, EDGE + HELD, EDGE)],
        [vmem(EDGE, EDGE), vmem(HELD, EDGE), vmem(EDGE, EDGE), vmem(HELD, EDGE), vmem(EDGE + HELD, EDGE), dma((3 + 2 * every,))],
        in_specs=[away], out_specs=[away, away],
    )(blocks)
    later, c0 = lax.optimization_barrier((blocks, c0))
    got0 = lax.all_to_all(c0, ("row", "col"), 0, 0, tiled=True)
    ar, ac = call(
        extract_kernel, [shape(NPAN, REST, EDGE, EDGE), shape(NPAN, EDGE, ROWS)],
        [vmem(NPAN, REST, EDGE, EDGE), vmem(NPAN, EDGE, ROWS), dma((NPAN + NPAN * REST,))],
        in_specs=[away], out_specs=[away, away],
    )(later)
    ar = lax.all_gather(ar, "col", axis=0)
    c1, ac, got0 = lax.optimization_barrier((c1, ac, got0))
    got1 = lax.all_to_all(c1, ("row", "col"), 0, 0, tiled=True)
    low0, inv0 = call(first_kernel, [square] * 2, work, out_specs=[away] * 2)(got0)
    later, got1, inv0 = lax.optimization_barrier((ac, got1, inv0))
    acs = [ac] + [lax.ppermute(piece, "row", [(i, (i + s) % GROUPS) for i in range(GROUPS)])
                  for s, piece in ((1, ac), (3, later), (2, later))]
    across, low1, inv1 = call(
        second_kernel, [square] * 3,
        work + [vmem(every, EDGE, EDGE), vmem(every, HELD, EDGE), vmem(WIDTH, WIDTH), vmem(WIDTH, WIDTH), dma((4,))],
        in_specs=[away] * 2, out_specs=[away] * 3,
    )(got1, inv0)
    whole, scalars = pl.BlockSpec(memory_space=pltpu.VMEM), pl.BlockSpec(memory_space=pltpu.SMEM)
    tall, flat, bound = [(NPAN, ROWS, WIDTH)] * 2, [(NPAN, WIDTH, ROWS)] * 2, [vmem(WIDTH, WIDTH, dtype=BF16)] * 2
    xh, xl, own_cols = call(
        row_kernel, [jax.ShapeDtypeStruct(dims, BF16) for dims in tall] + [shape(NPAN, ROWS, EDGE)],
        [vmem(GROUPS, NPAN, REST, EDGE, EDGE)] + [vmem(*dims, dtype=BF16) for dims in tall]
        + [vmem(ROWS, WIDTH, dtype=BF16)] * 2 + bound
        + [vmem(ROWS, WIDTH), vmem(NPAN, ROWS, EDGE), pltpu.SMEM((32,), jnp.int32), dma((NPAN,)), dma((3 * NPAN,))],
        in_specs=[away, scalars] + [whole] * 3, out_specs=[away] * 3,
    )(ar, pattern, inv0, across, inv1)
    result = call(
        last_kernel, shape(LB, EDGE, LB, EDGE),
        [vmem(LB, EDGE, LB, EDGE), vmem(GROUPS, NPAN, EDGE, ROWS)] + [vmem(*dims, dtype=BF16) for dims in tall + flat]
        + [vmem(WIDTH, ROWS, dtype=BF16)] * 2 + bound
        + [vmem(NPAN, ROWS, EDGE), vmem(WIDTH, ROWS), pltpu.SMEM((128,), jnp.int32), dma((24,)), dma((2,))],
        in_specs=[away, scalars] + [away] * 7 + [whole] * 5, out_specs=away,
    )(blocks, pattern, xh, xl, own_cols, *acs, low0, inv0, across, low1, inv1)
    return result[None, :, :, None]


def solution(mesh):
    placed = (P("row", "front", None, "col", None, None), P("front", None, None))
    return jax.shard_map(
        per_device, mesh=mesh, in_specs=placed,
        out_specs=P("row", "front", None, "col", None, None), check_vma=False,
    )
```

```python
import functools

import jax
import jax.numpy as jnp
from jax import lax
from jax.experimental import pallas as pl
from jax.experimental.pallas import tpu as pltpu
from jax.sharding import PartitionSpec as P

F32 = jnp.float32
BF16 = jnp.bfloat16
HI = lax.Precision.HIGHEST
EDGE = 128
TILE = 8
HALF = EDGE // 2
HELD = HALF + TILE
GROUPS = 4
WIDTH = EDGE * GROUPS
LB = 8
BATCH = 4
NPAN = 2
REST = LB - NPAN
ROWS = REST * EDGE

NN = (((1,), (0,)), ((), ()))
NT = (((1,), (1,)), ((), ()))
TN = (((0,), (0,)), ((), ()))


def exact_dot(a, b, dims):
    return lax.dot_general(a, b, dims, precision=HI, preferred_element_type=F32)


def split2(x):
    high = x.astype(BF16)
    return high, (x - high.astype(F32)).astype(BF16)


def split3(x):
    high = x.astype(BF16)
    rest = x - high.astype(F32)
    mid = rest.astype(BF16)
    return high, mid, (rest - mid.astype(F32)).astype(BF16)


def dot3(a, b, dims):
    one = functools.partial(lax.dot_general, dimension_numbers=dims, preferred_element_type=F32)
    return one(a[0], b[0]) + (one(a[0], b[1]) + one(a[1], b[0]))


def spread(x):
    return jnp.broadcast_to(x, (TILE, EDGE))


def factor_block(a, w):
    sub = lax.broadcasted_iota(jnp.int32, (TILE, EDGE), 0)
    count = EDGE // TILE

    def tile(p):
        return slice(TILE * p, TILE * (p + 1))

    def columns(x, p):
        return [spread(x[:, TILE * p + q:TILE * p + q + 1]) for q in range(TILE)]

    rows = [(a[tile(p), :], w[tile(p), :]) for p in range(2)]
    cols = columns(rows[0][0], 0)
    for p in range(count):
        if p + 2 < count:
            rows.append((a[tile(p + 2), :], w[tile(p + 2), :]))
        below = [columns(left, p) for left, _ in rows[1:]]
        corner = columns(rows[1][0], p + 1) if len(rows) > 1 else None
        invs = jnp.zeros((TILE, EDGE), F32)
        pivot = spread(cols[0][:1, :])
        for q in range(TILE):
            inv = 1.0 / pivot
            if q + 1 < TILE:
                beside = spread(cols[q + 1][q:q + 1, :])
                pivot = spread(cols[q + 1][q + 1:q + 2, :]) - (beside * beside) * inv
            invs = jnp.where(sub == q, inv, invs)
            factors = [jnp.where(sub > q, cols[q], 0.0) * inv] + [one[q] * inv for one in below]
            left, right = (spread(x[q:q + 1, :]) for x in rows[0])
            rows = [(x - m * left, y - m * right) for (x, y), m in zip(rows, factors)]
            if corner is not None:
                corner = [x - factors[1] * spread(below[0][q][t:t + 1, :]) for t, x in enumerate(corner)]
            for t in range(q + 1, TILE):
                across = spread(cols[t][q:q + 1, :])
                for one, m in zip([cols] + below, factors):
                    one[t] = one[t] - m * across
        root = lax.rsqrt(invs) * invs
        left, right = rows[0][0] * root, rows[0][1] * root
        a[tile(p), :], w[tile(p), :] = left, right
        low = TILE * (p + 3)
        if low < EDGE:
            h, m, l = split3(left)
            vh, vm, vl = split3(right)
            uh, um, ul = (jnp.concatenate(pair, 1) for pair in ((h, vh), (m, vm), (l, vl)))
            lhs = jnp.concatenate([h, h, m, h, m, l], 0)
            rhs = jnp.concatenate([uh, um, uh, ul, um, uh], 0)
            change = lax.dot_general(lhs, rhs, TN, preferred_element_type=F32)
            a[low:, :] = a[low:, :] - change[low:, :EDGE]
            w[low:, :] = w[low:, :] - change[low:, EDGE:]
        rows, cols = rows[1:], corner


def factor_panel(s, lower, inverse, a, w, low_out, inv_out, sem):
    ri = lax.broadcasted_iota(jnp.int32, (EDGE, EDGE), 0)
    ci = lax.broadcasted_iota(jnp.int32, (EDGE, EDGE), 1)
    copies = []
    for k in range(GROUPS):
        here = slice(k * EDGE, (k + 1) * EDGE)
        below = slice((k + 1) * EDGE, WIDTH)
        before = slice(0, k * EDGE)
        if k + 1 < GROUPS:
            lower[here, below] = jnp.zeros((EDGE, WIDTH - (k + 1) * EDGE), F32)
            inverse[here, below] = jnp.zeros((EDGE, WIDTH - (k + 1) * EDGE), F32)
        a[k] = s[here, here]
        w[k] = jnp.where(ri == ci, 1.0, 0.0)
        factor_block(a.at[k], w.at[k])
        d = w[k]
        if k + 1 < GROUPS:
            part = exact_dot(s[below, here], d, NT)
            lower[below, here] = part
            s[below, below] = s[below, below] - exact_dot(part, part, NT)
        lower[here, here] = jnp.where(ri <= ci, a[k], 0.0).T
        inverse[here, here] = d
        if k > 0:
            part = exact_dot(lower[here, before], inverse[before, before], NN)
            inverse[here, before] = -exact_dot(d, part, NN)
        for i, (held, to) in enumerate(((lower, low_out), (inverse, inv_out))):
            copies.append(pltpu.make_async_copy(held.at[here], to.at[here], sem.at[2 * k + i]))
            copies[-1].start()
    for copy in copies:
        copy.wait()


def pack(block, ref, r, c):
    row = lax.broadcasted_iota(jnp.int32, (HALF, EDGE), 0)
    lane = lax.broadcasted_iota(jnp.int32, (HALF, EDGE), 1)
    top, low = block[:HALF], block[HALF:]
    diagonal = jnp.where(lane - HALF > row, pltpu.roll(top, HALF, 1), low)
    ref[:HALF, :] = jnp.where(r == c, diagonal, jnp.where(r > c, top, block.T[HALF:]))
    ref[HALF:HELD, :] = spread(jnp.sum(jnp.where(lane == row, top, 0.0), axis=0, keepdims=True))


def unpack_diagonal(got):
    row = lax.broadcasted_iota(jnp.int32, (EDGE, EDGE), 0)
    lane = lax.broadcasted_iota(jnp.int32, (EDGE, EDGE), 1)
    body = got[:HALF]
    some = jnp.concatenate([pltpu.roll(body, HALF, 1), body], 0)
    kept = ((row >= HALF) & (lane <= row)) | ((lane < HALF) & (row < lane))
    whole = jnp.where(kept, some, some.T)
    return jnp.where((row == lane) & (row < HALF), jnp.broadcast_to(got[HALF:HALF + 1], (EDGE, EDGE)), whole)


def unpack(got, s):
    for r in range(GROUPS):
        for c in range(r):
            span = slice(c * EDGE, (c + 1) * EDGE)
            s[r * EDGE:r * EDGE + HALF, span] = got[r * GROUPS + c, 0:HALF]
            s[r * EDGE + HALF:(r + 1) * EDGE, span] = got[c * GROUPS + r, 0:HALF]
        span = slice(r * EDGE, (r + 1) * EDGE)
        s[span, span] = unpack_diagonal(got[r * GROUPS + r, 0:HELD])


def first_kernel(got, low_out, inv_out, s, lower, inverse, a, w, sem):
    unpack(got, s)
    factor_panel(s, lower, inverse, a, w, low_out, inv_out, sem)


def second_kernel(got, inverse0, across_out, low_out, inv_out, s, lower, inverse, a, w, sem, rect, square, across, invs, sem2):
    loads = [pltpu.make_async_copy(*pair, sem2.at[i]) for i, pair in enumerate(
        ((inverse0, invs), (got.at[:, :EDGE], rect), (got.at[:, EDGE:], square)))]
    for load in loads:
        load.start()
    loads[0].wait()
    inv = split2(invs[...])
    loads[1].wait()
    for r in range(GROUPS):
        for c in range(GROUPS):
            s[r * EDGE:(r + 1) * EDGE, c * EDGE:(c + 1) * EDGE] = rect[r * GROUPS + c]
    across[...] = dot3(split2(s[...]), inv, NT)
    store = pltpu.make_async_copy(across, across_out, sem2.at[3])
    store.start()
    loads[2].wait()
    unpack(square, s)
    part = split2(across[...])
    s[...] = s[...] - dot3(part, part, NT)
    factor_panel(s, lower, inverse, a, w, low_out, inv_out, sem)
    store.wait()


def collect(ids, at, flags):
    for number, flag in flags:
        ids[at] = number
        at = at + jnp.where(flag, 1, 0)
    return at


def visit(ids, first, last, product, target):
    def step(i, _):
        slots = [first + i * BATCH + j for j in range(BATCH)]
        numbers = [ids[jnp.minimum(slot, last - 1)] for slot in slots]
        changes = [jnp.where(slot < last, product(number), 0.0) for slot, number in zip(slots, numbers)]
        for number, change in zip(numbers, changes):
            target(number, change)
        return 0

    lax.fori_loop(0, lax.div(last - first + BATCH - 1, BATCH), step, 0)


def spans(i):
    return pl.ds(pl.multiple_of(i * EDGE, EDGE), EDGE)


def unpair(number):
    return lax.div(number, TILE), lax.rem(number, TILE)


SIDE = [(l, g) for l in range(REST) for g in range(GROUPS)]


def row_kernel(ar, pattern, inv0, across, inv1, xh_out, xl_out, mine_out,
               arv, xh, xl, th, tl, bh, bl, lr, mine, ids, arrive, leave):
    r, own = lax.axis_index("row"), spans(lax.axis_index("col"))
    half = WIDTH // 2
    loads = [pltpu.make_async_copy(ar.at[:, k], arv.at[:, k], arrive.at[k]) for k in range(NPAN)]
    for load in loads:
        load.start()
    bh[...], bl[...] = split2(across[...])
    end = collect(ids, 0, [(l * TILE + g, pattern[0, (l + NPAN) * GROUPS + r, GROUPS + g] > 0) for l, g in SIDE])

    def product(number):
        l, g = unpair(number)
        return dot3((xh[0, spans(l), :], xl[0, spans(l), :]), (bh[spans(g), :], bl[spans(g), :]), NT)

    def target(number, change):
        l, g = unpair(number)
        arv[g, 1, l] = arv[g, 1, l] - change

    stores = []
    for k in range(NPAN):
        loads[k].wait()
        if k == 1:
            visit(ids, 0, end, product, target)
        for g in range(GROUPS):
            span = slice(g * EDGE, (g + 1) * EDGE)
            th[:, span], tl[:, span] = split2(arv[g, k].reshape(ROWS, EDGE))
        wh, wl = split2((inv0, inv1)[k][...])
        lr[:, :half] = dot3((th[:, :half], tl[:, :half]), (wh[:half, :half], wl[:half, :half]), NT)
        lr[:, half:] = dot3((th[...], tl[...]), (wh[half:, :], wl[half:, :]), NT)
        xh[k], xl[k] = split2(lr[...])
        mine[k] = lr[:, own]
        for i, (held, to) in enumerate(((xh, xh_out), (xl, xl_out), (mine, mine_out))):
            stores.append(pltpu.make_async_copy(held.at[k], to.at[k], leave.at[3 * k + i]))
            stores[-1].start()
    for store in stores:
        store.wait()


def last_kernel(front, pattern, xh_in, xl_in, own_cols, ac0, ac1, ac3, ac2, low0, inv0, across, low1, inv1, out,
                buf, acv, xh, xl, yh, yl, sh, sl, bh, bl, held, lc, ids, arrive, leave):
    r, c = lax.axis_index("row"), lax.axis_index("col")
    own, mine = spans(c), spans(r)
    half = WIDTH // 2
    loads = []
    for k in range(NPAN):
        loads.append([pltpu.make_async_copy(ac.at[k], acv.at[(r + GROUPS - s) % GROUPS, k], arrive.at[4 * k + s])
                      for s, ac in ((0, ac0), (1, ac1), (2, ac2), (3, ac3))])
    copies = [pltpu.make_async_copy(*pair, arrive.at[8 + i])
              for i, pair in enumerate(((own_cols, held), (xh_in, xh), (xl_in, xl)))]
    fronts = [pltpu.make_async_copy(front.at[l], buf.at[l], arrive.at[16 + l]) for l in range(NPAN, LB)]
    for load in loads[0] + loads[1] + copies + fronts:
        load.start()
    zero = jnp.zeros((EDGE, EDGE), F32)
    for l in range(NPAN):
        for m in range(NPAN, LB):
            buf[l, :, m, :] = zero
    buf[0, :, 1, :] = zero
    buf[0, :, 0, :] = low0[mine, own]
    buf[1, :, 0, :] = across[mine, own]
    buf[1, :, 1, :] = low1[mine, own]
    store = pltpu.make_async_copy(buf.at[:NPAN], out.at[:NPAN], leave.at[0])
    store.start()
    bh[...], bl[...] = split2(across[...])
    col_end = collect(ids, 0, [(l * TILE + g, pattern[0, GROUPS + g, (l + NPAN) * GROUPS + c] > 0) for l, g in SIDE])
    all_end = collect(ids, col_end, [
        ((k * TILE + l) * TILE + m, pattern[k, (l + NPAN) * GROUPS + r, (m + NPAN) * GROUPS + c] > 0)
        for k in range(NPAN) for l in range(REST) for m in range(REST)])

    def col_product(number):
        l, g = unpair(number)
        return dot3((bh[spans(g), :], bl[spans(g), :]), (yh[0, :, spans(l)], yl[0, :, spans(l)]), NN)

    def col_target(number, change):
        l, g = unpair(number)
        acv[g, 1, :, spans(l)] = acv[g, 1, :, spans(l)] - change

    def place(number):
        row, m = unpair(number)
        return unpair(row) + (m,)

    def product(number):
        k, l, m = place(number)
        return dot3((xh[k, spans(l), :], xl[k, spans(l), :]), (yh[k, :, spans(m)], yl[k, :, spans(m)]), NN)

    def target(number, change):
        k, l, m = place(number)
        buf[l + NPAN, :, m + NPAN, :] = buf[l + NPAN, :, m + NPAN, :] - change

    for k in range(NPAN):
        for load in loads[k]:
            load.wait()
        if k == 1:
            visit(ids, 0, col_end, col_product, col_target)
        for g in range(GROUPS):
            span = slice(g * EDGE, (g + 1) * EDGE)
            sh[span, :], sl[span, :] = split2(acv[g, k])
        wh, wl = split2((inv0, inv1)[k][...])
        lc[:half, :] = dot3((wh[:half, :half], wl[:half, :half]), (sh[:half, :], sl[:half, :]), NN)
        lc[half:, :] = dot3((wh[half:, :], wl[half:, :]), (sh[...], sl[...]), NN)
        yh[k], yl[k] = split2(lc[...])
    for load in copies + fronts:
        load.wait()
    for k in range(NPAN):
        for l in range(REST):
            buf[l + NPAN, :, k, :] = held[k, l * EDGE:(l + 1) * EDGE, :]
    visit(ids, col_end, all_end, product, target)
    last = pltpu.make_async_copy(buf.at[NPAN:], out.at[NPAN:], leave.at[1])
    last.start()
    store.wait()
    last.wait()


def run(copies):
    for copy in copies:
        copy.start()
    for copy in copies:
        copy.wait()


def extract_kernel(front, ar, ac, rows, cols, sem):
    copy = pltpu.make_async_copy
    loads = [copy(front.at[NPAN:, :, k, :], rows.at[k], sem.at[k]) for k in range(NPAN)]
    for k in range(NPAN):
        for j in range(REST):
            loads.append(copy(front.at[k, :, j + NPAN, :], cols.at[k, :, j * EDGE:(j + 1) * EDGE], sem.at[len(loads)]))
    run(loads)
    run([copy(rows, ar, sem.at[0]), copy(cols, ac, sem.at[1])])


def corner_kernel(front, c0, c1, first, second, third, send0, send1, sem):
    r, c = lax.axis_index("row"), lax.axis_index("col")
    copy = pltpu.make_async_copy
    every = GROUPS * GROUPS
    loads = [copy(front.at[l, :, m, :], to, sem.at[i])
             for i, (l, m, to) in enumerate(((0, 0, first), (1, 0, send1.at[:EDGE]), (1, 1, third)))]
    for one in loads:
        one.start()
    loads[0].wait()
    pack(first[...], send0, r, c)
    stores = [copy(send0, c0.at[g], sem.at[3 + g]) for g in range(every)]
    for one in stores:
        one.start()
    loads[1].wait()
    loads[2].wait()
    pack(third[...], second, r, c)
    send1[EDGE:, :] = second[...]
    last = [copy(send1, c1.at[g], sem.at[3 + every + g]) for g in range(every)]
    for one in last:
        one.start()
    for one in stores + last:
        one.wait()


def shape(*dims):
    return jax.ShapeDtypeStruct(dims, F32)


def vmem(*dims, dtype=F32):
    return pltpu.VMEM(dims, dtype)


def call(kernel, outs, scratch=(), limit=60, **kw):
    return pl.pallas_call(
        kernel, out_shape=outs, scratch_shapes=list(scratch),
        compiler_params=pltpu.CompilerParams(vmem_limit_bytes=limit * 1024 * 1024), **kw)


def per_device(front, pattern):
    blocks = front[0, :, :, 0]
    square = shape(WIDTH, WIDTH)
    every = GROUPS * GROUPS
    away, dma = pl.BlockSpec(memory_space=pltpu.HBM), pltpu.SemaphoreType.DMA
    work = [vmem(WIDTH, WIDTH)] * 3 + [vmem(GROUPS, EDGE, EDGE)] * 2 + [dma((LB,))]
    c0, c1 = call(
        corner_kernel, [shape(every, HELD, EDGE), shape(every, EDGE + HELD, EDGE)],
        [vmem(EDGE, EDGE), vmem(HELD, EDGE), vmem(EDGE, EDGE), vmem(HELD, EDGE), vmem(EDGE + HELD, EDGE), dma((3 + 2 * every,))],
        in_specs=[away], out_specs=[away, away],
    )(blocks)
    later, c0 = lax.optimization_barrier((blocks, c0))
    got0 = lax.all_to_all(c0, ("row", "col"), 0, 0, tiled=True)
    ar, ac = call(
        extract_kernel, [shape(NPAN, REST, EDGE, EDGE), shape(NPAN, EDGE, ROWS)],
        [vmem(NPAN, REST, EDGE, EDGE), vmem(NPAN, EDGE, ROWS), dma((NPAN + NPAN * REST,))],
        in_specs=[away], out_specs=[away, away],
    )(later)
    ar = lax.all_gather(ar, "col", axis=0)
    c1, got0 = lax.optimization_barrier((c1, got0))
    got1 = lax.all_to_all(c1, ("row", "col"), 0, 0, tiled=True)
    low0, inv0 = call(first_kernel, [square] * 2, work, out_specs=[away] * 2)(got0)
    later, inv0 = lax.optimization_barrier((ac, inv0))
    acs = [ac] + [lax.ppermute(piece, "row", [(i, (i + s) % GROUPS) for i in range(GROUPS)])
                  for s, piece in ((1, later), (3, later), (2, later))]
    across, low1, inv1 = call(
        second_kernel, [square] * 3,
        work + [vmem(every, EDGE, EDGE), vmem(every, HELD, EDGE), vmem(WIDTH, WIDTH), vmem(WIDTH, WIDTH), dma((4,))],
        in_specs=[away] * 2, out_specs=[away] * 3,
    )(got1, inv0)
    whole, scalars = pl.BlockSpec(memory_space=pltpu.VMEM), pl.BlockSpec(memory_space=pltpu.SMEM)
    tall, flat, bound = [(NPAN, ROWS, WIDTH)] * 2, [(NPAN, WIDTH, ROWS)] * 2, [vmem(WIDTH, WIDTH, dtype=BF16)] * 2
    xh, xl, own_cols = call(
        row_kernel, [jax.ShapeDtypeStruct(dims, BF16) for dims in tall] + [shape(NPAN, ROWS, EDGE)],
        [vmem(GROUPS, NPAN, REST, EDGE, EDGE)] + [vmem(*dims, dtype=BF16) for dims in tall]
        + [vmem(ROWS, WIDTH, dtype=BF16)] * 2 + bound
        + [vmem(ROWS, WIDTH), vmem(NPAN, ROWS, EDGE), pltpu.SMEM((32,), jnp.int32), dma((NPAN,)), dma((3 * NPAN,))],
        in_specs=[away, scalars] + [whole] * 3, out_specs=[away] * 3,
    )(ar, pattern, inv0, across, inv1)
    result = call(
        last_kernel, shape(LB, EDGE, LB, EDGE),
        [vmem(LB, EDGE, LB, EDGE), vmem(GROUPS, NPAN, EDGE, ROWS)] + [vmem(*dims, dtype=BF16) for dims in tall + flat]
        + [vmem(WIDTH, ROWS, dtype=BF16)] * 2 + bound
        + [vmem(NPAN, ROWS, EDGE), vmem(WIDTH, ROWS), pltpu.SMEM((128,), jnp.int32), dma((24,)), dma((2,))],
        in_specs=[away, scalars] + [away] * 7 + [whole] * 5, out_specs=away,
    )(blocks, pattern, xh, xl, own_cols, *acs, low0, inv0, across, low1, inv1)
    return result[None, :, :, None]


def solution(mesh):
    placed = (P("row", "front", None, "col", None, None), P("front", None, None))
    return jax.shard_map(
        per_device, mesh=mesh, in_specs=placed,
        out_specs=P("row", "front", None, "col", None, None), check_vma=False,
    )
```
